128 devices in a mesh: lat: 8 (over y_lo, x), lon: 16 (over y_hi, z, core).
Axes of the slice: x: 4, y: 4 (y_hi: 2, y_lo: 2; y = y_hi * 2 + y_lo), z: 4, core: 2. Of those that a mesh axis runs over, the one named last changes fastest.
Arguments:
- inputs: bfloat16 [64, 2, 2, 192, 2048], P(None, None, None, 'lat', 'lon'), may hold values from -6 to 6
- kernels: float32 [2, 9, 128], replicated, may hold values from -0.6 to 0.6
- w_down: bfloat16 [9, 128, 64], replicated, may hold values from -0.25 to 0.25
- w_up: bfloat16 [9, 64, 128], replicated, may hold values from -0.3125 to 0.3125
- cotangent: bfloat16 [64, 2, 2, 192, 2048], P(None, None, None, 'lat', 'lon'), may hold values from -6 to 6
- coverage: int32 [24, 256], P('lat', 'lon'), may hold values 0 or 1
Outputs:
- decoded: bfloat16 [64, 2, 2, 192, 2048], P(None, None, None, 'lat', 'lon')
- grad_input: bfloat16 [64, 2, 2, 192, 2048], P(None, None, None, 'lat', 'lon')
- grad_down: float32 [9, 128, 64], replicated
- grad_up: float32 [9, 64, 128], replicated
- grad_kernels: float32 [2, 9, 128], P(None, None, ('lat', 'lon'))
The draws below stay inside these ranges and needn't reach their ends.
Inputs may be any that keep to these rules, and one draw needn't show every extreme that they name: 1 where the tile carries loss gradient, 0 where it has no swath coverage.
All inputs are finite; a program needn't handle non-finite values. No bound on the sum of `coverage` on one device may be relied on, other than what follows from the above.
Results may differ from the reference program's by a relative error of at most 0.012.
Values may be sent and summed in bfloat16 or wider, within the bound.
A program may use at most 128 MiB of HBM per device.

```python
import jax
import jax.numpy as jnp
from jax import lax

CH = 64
DEEP = 128
DWSTEPS = 2
TILE = 16
LAT = 384
LON = 4096


def set_ends(result, rng, least, largest):
    longest = result.shape.index(max(result.shape))
    spots = []
    for shift in (0, 1):
        where = [jax.random.randint(jax.random.fold_in(rng, axis), (), 0, length) for axis, length in enumerate(result.shape)]
        where[longest] = (where[longest] + shift) % result.shape[longest]
        spots.append(tuple(where))
    return result.at[spots[0]].set(least).at[spots[1]].set(largest)


def steps_of(key, extent, split, smallest, high):
    factor_of = 1.0
    for position, shards_of in split:
        draws = jax.random.uniform(jax.random.fold_in(jax.random.fold_in(key, 6), position), (shards_of,), jnp.float32, smallest / len(split), high / len(split))
        factor_of = factor_of * jnp.repeat(jnp.exp(draws), extent[position] // shards_of).reshape((-1,) + (1,) * (len(extent) - 1 - position))
    return factor_of


def centred(own_key, extent, scale, reach, shards=(), kind=jnp.bfloat16):
    values = scale * jax.random.normal(own_key, extent, jnp.float32)
    if shards:
        values = values * steps_of(own_key, extent, shards, -0.22, 0.18)
    return jnp.clip(values, -reach, reach).astype(kind)


def setup_inputs(seed: int = 0) -> dict:
    key_of = jax.random.split(jax.random.key(seed), 7)
    return {
        "inputs": centred(key_of[0], (CH, 2, 2, LAT // 2, LON // 2), 1.0, 6.0, ((3, 8), (4, 16))),
        "kernels": centred(key_of[1], (DWSTEPS, 9, DEEP), 0.2, 0.6, (), jnp.float32),
        "w_down": centred(key_of[2], (9, DEEP, CH), (9 * CH) ** -0.5, 0.25),
        "w_up": centred(key_of[3], (9, CH, DEEP), (3 * DEEP) ** -0.5, 0.3125),
        "cotangent": centred(key_of[4], (CH, 2, 2, LAT // 2, LON // 2), 1.0, 6.0, ((3, 8), (4, 16))),
        "coverage": set_ends((jax.random.randint(key_of[5], (LAT // TILE, LON // TILE), 0, 2) < 1).astype(jnp.int32), jax.random.fold_in(key_of[5], 1), 0, 1),
    }


HIGH = lax.Precision.HIGHEST

def rows_down(field):
    return jnp.concatenate([jnp.zeros_like(field[..., :1, :]), field[..., :-1, :]], axis=-2)

def rows_up(field):
    return jnp.concatenate([field[..., 1:, :], jnp.zeros_like(field[..., :1, :])], axis=-2)

def cols_right(field):
    return jnp.concatenate([field[..., -1:], field[..., :-1]], axis=-1)

def cols_left(field):
    return jnp.concatenate([field[..., 1:], field[..., :1]], axis=-1)

def plane_taps(planes):
    above = rows_down(planes[:, 1])
    sources = [above, planes[:, 0], planes[:, 1]]
    taps = []
    for src in sources:
        taps.append(cols_right(src[:, 1]))
        taps.append(src[:, 0])
        taps.append(src[:, 1])
    return taps

def wrap_ext(field, width):
    wide = jnp.concatenate([field[:, :, -width:], field, field[:, :, :width]], axis=2)
    return jnp.pad(wide, ((0, 0), (width, width), (0, 0)))

def conv_taps(weight, taps, form):
    total = 0.0
    for tap in range(9):
        total = total + jnp.einsum(form, weight[tap].astype(jnp.float32), taps[tap].astype(jnp.float32), precision=HIGH)
    return total

def up_conv(weight, deep, form):

    def mul(tap, value):
        return jnp.einsum(form, weight[tap].astype(jnp.float32), value.astype(jnp.float32), precision=HIGH)
    below = rows_up(deep)
    beside = cols_left(deep)
    corner = cols_left(below)
    even_even = mul(4, deep)
    even_odd = mul(5, deep) + mul(3, beside)
    odd_even = mul(7, deep) + mul(1, below)
    odd_odd = mul(8, deep) + mul(6, beside) + mul(2, below) + mul(0, corner)
    upper = jnp.stack([even_even, even_odd], axis=1)
    lower = jnp.stack([odd_even, odd_odd], axis=1)
    return jnp.stack([upper, lower], axis=1)

def crop(field, width):
    return field[:, width:field.shape[1] - width, width:field.shape[2] - width]

def row_mask(count, margin, start, total):
    rows = start - margin + jnp.arange(count, dtype=jnp.int32)
    return ((rows >= 0) & (rows < total)).astype(jnp.float32)[None, :, None]

def dw_forward(ext, kernels, start, total):
    steps = kernels.shape[0]
    states = [ext]
    current = ext
    for step in range(steps):
        rows = current.shape[1] - 2
        cols = current.shape[2] - 2
        acc = current[:, 1:-1, 1:-1]
        for a in range(3):
            for b in range(3):
                acc = acc + kernels[step, 3 * a + b][:, None, None] * current[:, a:a + rows, b:b + cols]
        current = acc * row_mask(rows, steps - step - 1, start, total)
        states.append(current)
    return states

def dw_backward(dext, kernels, states, start, total):
    steps = kernels.shape[0]
    current = dext
    grads = []
    for step in reversed(range(steps)):
        rows = current.shape[1] - 2
        cols = current.shape[2] - 2
        inner = crop(current, step + 1)
        state = crop(states[step], steps - step - 1)
        count_r = inner.shape[1]
        count_c = inner.shape[2]
        terms = []
        for a in range(3):
            for b in range(3):
                terms.append(lax.optimization_barrier(jnp.sum(inner * state[:, a:a + count_r, b:b + count_c], axis=(1, 2))))
        grads.insert(0, jnp.stack(terms, axis=0))
        acc = current[:, 1:-1, 1:-1]
        for a in range(3):
            for b in range(3):
                acc = acc + kernels[step, 3 * a + b][:, None, None] * current[:, 2 - a:2 - a + rows, 2 - b:2 - b + cols]
        current = acc * row_mask(rows, step, start, total)
    return (current, jnp.stack(grads, axis=0))

def reference(inputs, kernels, w_down, w_up, cotangent, coverage):
    rows2 = inputs.shape[3]
    cols2 = inputs.shape[4]
    steps = kernels.shape[0]
    scale = 1.0 / jnp.sqrt(jnp.float32(rows2 * cols2))
    in_taps = plane_taps(inputs)
    pre = conv_taps(w_down, in_taps, 'oc,crw->orw')
    hidden = jax.nn.silu(pre).astype(jnp.bfloat16)
    states = dw_forward(wrap_ext(hidden.astype(jnp.float32), steps), kernels, 0, rows2)
    deep_out = states[-1].astype(jnp.bfloat16)
    decoded = (inputs.astype(jnp.float32) + up_conv(w_up, deep_out, 'co,orw->crw')).astype(jnp.bfloat16)
    half_r = rows2 // coverage.shape[0]
    half_c = cols2 // coverage.shape[1]
    flags = jnp.repeat(jnp.repeat(coverage, half_r, axis=0), half_c, axis=1).astype(jnp.bfloat16)
    masked = cotangent * flags[None, None, None]
    dy_taps = plane_taps(masked)
    deep_grad = conv_taps(w_up, dy_taps, 'co,crw->orw').astype(jnp.bfloat16)
    grad_up = jnp.stack([jnp.einsum('crw,orw->co', tap.astype(jnp.float32), deep_out.astype(jnp.float32), precision=HIGH) for tap in dy_taps], axis=0) * scale
    hidden_grad, kernel_term = dw_backward(wrap_ext(deep_grad.astype(jnp.float32), steps), kernels, states, 0, rows2)
    hidden_grad = hidden_grad.astype(jnp.bfloat16)
    sig = jax.nn.sigmoid(pre)
    pre_grad = (hidden_grad.astype(jnp.float32) * sig * (1.0 + pre * (1.0 - sig))).astype(jnp.bfloat16)
    back = up_conv(w_down, pre_grad, 'oc,orw->crw')
    grad_input = (masked.astype(jnp.float32) + back).astype(jnp.bfloat16)
    grad_down = jnp.stack([jnp.einsum('orw,crw->oc', pre_grad.astype(jnp.float32), tap.astype(jnp.float32), precision=HIGH) for tap in in_taps], axis=0) * scale
    return (decoded, grad_input, grad_down, grad_up, kernel_term * scale)
```

```python
import functools
import math

import jax
import jax.numpy as jnp
from jax import lax
from jax.experimental import pallas as pl
from jax.experimental.pallas import tpu as pltpu
from jax.sharding import PartitionSpec as P


def shifted(block, axis, distance):
    devices = range(lax.axis_size(axis))
    route = [(i - distance, i) for i in devices if i - distance in devices]
    return lax.ppermute(block, axis, route)


def shifted_2(value, axis, steps):
    count = lax.axis_size(axis)
    pairs = [(source, (source + steps) % count) for source in range(count)]
    return lax.ppermute(value, axis, pairs)


def lat_rim(piece, shift_by):
    return shifted(piece, "lat", shift_by)


def lon_rim(piece, shift_by):
    return shifted_2(piece, "lon", shift_by)


def plane_taps(planes):
    upper = planes[:, 1]
    above = jnp.concatenate([lat_rim(upper[..., -1:, :], 1), upper[..., :-1, :]], axis=-2)
    sources = [above, planes[:, 0], planes[:, 1]]
    rims = lon_rim(jnp.stack([src[:, 1, :, -1:] for src in sources], axis=0), 1)
    taps = []
    for index in range(3):
        src = sources[index]
        taps.append(jnp.concatenate([rims[index], src[:, 1, :, :-1]], axis=-1))
        taps.append(src[:, 0])
        taps.append(src[:, 1])
    return taps


def margin_ext(field, width):
    wide = jnp.concatenate(
        [lon_rim(field[:, :, -width:], 1), field, lon_rim(field[:, :, :width], -1)], axis=2
    )
    return jnp.concatenate(
        [lat_rim(wide[:, -width:, :], 1), wide, lat_rim(wide[:, :width, :], -1)], axis=1
    )


def conv_taps(weight, taps, form):
    total = 0.0
    for tap in range(9):
        total = total + jnp.einsum(form, weight[tap], taps[tap], preferred_element_type=jnp.float32)
    return total


def up_conv(weight, deep, form):

    def mul(tap, value):
        return jnp.einsum(form, weight[tap], value, preferred_element_type=jnp.float32)

    below = jnp.concatenate([deep[:, 1:, :], lat_rim(deep[:, :1, :], -1)], axis=1)
    rims = lon_rim(jnp.stack([deep[:, :, :1], below[:, :, :1]], axis=0), -1)
    beside = jnp.concatenate([deep[:, :, 1:], rims[0]], axis=2)
    corner = jnp.concatenate([below[:, :, 1:], rims[1]], axis=2)
    even_even = mul(4, deep)
    even_odd = mul(5, deep) + mul(3, beside)
    odd_even = mul(7, deep) + mul(1, below)
    odd_odd = mul(8, deep) + mul(6, beside) + mul(2, below) + mul(0, corner)
    upper = jnp.stack([even_even, even_odd], axis=1)
    lower = jnp.stack([odd_even, odd_odd], axis=1)
    return jnp.stack([upper, lower], axis=1)


def crop(field, width):
    return field[:, width : field.shape[1] - width, width : field.shape[2] - width]


def row_mask(count, margin, start, total):
    rows = start - margin + jnp.arange(count, dtype=jnp.int32)
    return ((rows >= 0) & (rows < total)).astype(jnp.float32)[None, :, None]


def dw_forward(ext, kernels, start, total):
    steps = kernels.shape[0]
    states = [ext]
    current = ext
    for step in range(steps):
        rows = current.shape[1] - 2
        cols = current.shape[2] - 2
        acc = current[:, 1:-1, 1:-1]
        for a in range(3):
            for b in range(3):
                acc = (
                    acc
                    + kernels[step, 3 * a + b][:, None, None]
                    * current[:, a : a + rows, b : b + cols]
                )
        current = acc * row_mask(rows, steps - step - 1, start, total)
        states.append(current)
    return states


def dw_backward(dext, kernels, states, start, total):
    steps = kernels.shape[0]
    current = dext
    grads = []
    for step in reversed(range(steps)):
        rows = current.shape[1] - 2
        cols = current.shape[2] - 2
        inner = crop(current, step + 1)
        state = crop(states[step], steps - step - 1)
        count_r = inner.shape[1]
        count_c = inner.shape[2]
        terms = []
        for a in range(3):
            for b in range(3):
                terms.append(
                    jnp.sum(inner * state[:, a : a + count_r, b : b + count_c], axis=(1, 2))
                )
        grads.insert(0, jnp.stack(terms, axis=0))
        acc = current[:, 1:-1, 1:-1]
        for a in range(3):
            for b in range(3):
                acc = (
                    acc
                    + kernels[step, 3 * a + b][:, None, None]
                    * current[:, 2 - a : 2 - a + rows, 2 - b : 2 - b + cols]
                )
        current = acc * row_mask(rows, step, start, total)
    return (current, jnp.stack(grads, axis=0))


MESH = pl.DeviceIdType.MESH
N_LAT = 8
N_LON = 16
PIECE = 36
PADDED = 48


def send(src, dst, send_sem, recv_sem, target):
    return pltpu.make_async_remote_copy(
        src_ref=src,
        dst_ref=dst,
        send_sem=send_sem,
        recv_sem=recv_sem,
        device_id=target,
        device_id_type=MESH,
    )


def greet(my_lat, my_lon):
    barrier = pltpu.get_barrier_semaphore()
    for d in range(1, N_LON):
        pl.semaphore_signal(
            barrier, inc=1, device_id=(my_lat, lax.rem(my_lon + d, N_LON)), device_id_type=MESH
        )
    for d in range(1, N_LAT):
        pl.semaphore_signal(
            barrier, inc=1, device_id=(lax.rem(my_lat + d, N_LAT), my_lon), device_id_type=MESH
        )
    pl.semaphore_wait(barrier, N_LON + N_LAT - 2)


class Sum:
    def __init__(self, my_lat, my_lon, pieces, got, part, parts, whole, sems):
        self.my_lat, self.my_lon = my_lat, my_lon
        self.pieces, self.got, self.part, self.parts, self.whole = pieces, got, part, parts, whole
        self.s1, self.r1, self.s2, self.r2, self.s3, self.r3 = sems

    def lon_peer(self, d):
        return (self.my_lat, lax.rem(self.my_lon + d, N_LON))

    def lat_peer(self, d):
        return (lax.rem(self.my_lat + d, N_LAT), self.my_lon)

    def first(self, d):
        peer = lax.rem(self.my_lon + d, N_LON)
        return send(self.pieces.at[peer], self.got.at[d], self.s1.at[d], self.r1.at[d], self.lon_peer(d))

    def second(self, d):
        return send(self.part, self.parts.at[self.my_lat], self.s2.at[d], self.r2.at[d], self.lat_peer(d))

    def third(self, d):
        mine = self.whole.at[self.my_lon]
        return send(mine, mine, self.s3.at[d], self.r3.at[d], self.lon_peer(d))

    def start_first(self):
        for d in range(1, N_LON):
            self.first(d).start()

    def start_second(self):
        total = self.pieces[self.my_lon].astype(jnp.float32)
        for d in range(1, N_LON):
            self.first(d).wait_recv()
            total = total + self.got[d].astype(jnp.float32)
        rounded = total.astype(jnp.bfloat16)
        self.part[...] = rounded
        self.parts[self.my_lat] = rounded
        for d in range(1, N_LAT):
            self.second(d).start()

    def start_third(self):
        for d in range(1, N_LAT):
            self.second(d).wait_recv()
        total = self.parts[0].astype(jnp.float32)
        for lat in range(1, N_LAT):
            total = total + self.parts[lat].astype(jnp.float32)
        self.whole[self.my_lon] = total.astype(jnp.bfloat16)
        for d in range(1, N_LON):
            self.third(d).start()

    def finish(self, scale, out):
        for d in range(1, N_LON):
            self.third(d).wait_recv()
        for k in range(N_LON):
            piece = self.whole[k].astype(jnp.float32)[:PIECE] * scale
            out[pl.ds(k * PIECE, PIECE), :] = piece
        for d in range(1, N_LON):
            self.first(d).wait_send()
            self.third(d).wait_send()
        for d in range(1, N_LAT):
            self.second(d).wait_send()


class Small(Sum):
    def __init__(self, my_lat, my_lon, mine, got, part, parts, sems):
        self.my_lat, self.my_lon = my_lat, my_lon
        self.mine, self.got, self.part, self.parts = mine, got, part, parts
        self.s1, self.r1, self.s2, self.r2 = sems

    def first(self, d):
        return send(self.mine, self.got.at[d], self.s1.at[d], self.r1.at[d], self.lon_peer(d))

    def start_second(self):
        total = self.mine[...]
        for d in range(1, N_LON):
            self.first(d).wait_recv()
            total = total + self.got[d]
        self.part[...] = total
        for d in range(1, N_LAT):
            self.second(d).start()

    def second(self, d):
        return send(self.part, self.parts.at[d], self.s2.at[d], self.r2.at[d], self.lat_peer(d))

    def finish(self, scale, out):
        total = self.part[...]
        for d in range(1, N_LAT):
            self.second(d).wait_recv()
            total = total + self.parts[d]
        lane = lax.broadcasted_iota(jnp.int32, total.shape, 1)
        mine = lane == self.my_lat * N_LON + self.my_lon
        out[...] = jnp.sum(jnp.where(mine, total, 0.0), axis=1, keepdims=True) * scale
        for d in range(1, N_LON):
            self.first(d).wait_send()
        for d in range(1, N_LAT):
            self.second(d).wait_send()


def sum_scratch():
    return [
        pltpu.VMEM((N_LON, PADDED, 128), jnp.bfloat16),
        pltpu.VMEM((N_LON, PADDED, 128), jnp.bfloat16),
        pltpu.VMEM((PADDED, 128), jnp.bfloat16),
        pltpu.VMEM((N_LAT, PADDED, 128), jnp.bfloat16),
        pltpu.VMEM((N_LON, PADDED, 128), jnp.bfloat16),
    ] + [pltpu.SemaphoreType.DMA((n,)) for n in (N_LON, N_LON, N_LAT, N_LAT, N_LON, N_LON)]


def small_scratch(shape):
    return [
        pltpu.VMEM((N_LON,) + shape, jnp.float32),
        pltpu.VMEM(shape, jnp.float32),
        pltpu.VMEM((N_LAT,) + shape, jnp.float32),
    ] + [pltpu.SemaphoreType.DMA((n,)) for n in (N_LON, N_LON, N_LAT, N_LAT)]


def sum_kernel(scale, down_ref, up_ref, small_ref, down_out, up_out, small_out, *scratch):
    my_lat, my_lon = lax.axis_index("lat"), lax.axis_index("lon")
    greet(my_lat, my_lon)
    down = Sum(my_lat, my_lon, *scratch[:5], scratch[5:11])
    up = Sum(my_lat, my_lon, *scratch[11:16], scratch[16:22])
    small = Small(my_lat, my_lon, small_ref, *scratch[22:25], scratch[25:29])
    for each, source in ((down, down_ref), (up, up_ref)):
        for k in range(N_LON):
            each.pieces[k] = source[pl.ds(k * PIECE, PADDED), :].astype(jnp.bfloat16)
        each.start_first()
    small.start_first()
    down.start_second()
    up.start_second()
    small.start_second()
    down.start_third()
    up.start_third()
    down.finish(scale, down_out)
    up.finish(scale, up_out)
    small.finish(scale, small_out)


def all_sums(down, up, small, scale):
    pad = PADDED - PIECE
    full = pl.BlockSpec(memory_space=pltpu.VMEM)
    return pl.pallas_call(
        functools.partial(sum_kernel, scale),
        out_shape=(
            jax.ShapeDtypeStruct((576, 128), jnp.float32),
            jax.ShapeDtypeStruct((576, 128), jnp.float32),
            jax.ShapeDtypeStruct((24, 1), jnp.float32),
        ),
        in_specs=[full] * 3,
        out_specs=(full,) * 3,
        scratch_shapes=sum_scratch() + sum_scratch() + small_scratch((24, 128)),
        compiler_params=pltpu.CompilerParams(
            collective_id=0, has_side_effects=True, vmem_limit_bytes=16 * 1024 * 1024
        ),
    )(
        jnp.pad(down.reshape(576, 128), ((0, pad), (0, 0))),
        jnp.pad(up.reshape(576, 128), ((0, pad), (0, 0))),
        jnp.pad(small.reshape(18, 128), ((0, 6), (0, 0))),
    )


def shards(inputs, kernels, w_down, w_up, cotangent, coverage):
    rows2 = inputs.shape[3]
    cols2 = inputs.shape[4]
    steps = kernels.shape[0]
    n_lat = lax.axis_size("lat")
    n_lon = lax.axis_size("lon")
    total2 = rows2 * n_lat
    scale = 1.0 / math.sqrt(total2 * cols2 * n_lon)
    in_taps = plane_taps(inputs)
    pre = conv_taps(w_down, in_taps, "oc,crw->orw")
    hidden = jax.nn.silu(pre).astype(jnp.bfloat16)
    start = lax.axis_index("lat") * rows2
    states = dw_forward(margin_ext(hidden, steps).astype(jnp.float32), kernels, start, total2)
    deep_out = states[-1].astype(jnp.bfloat16)
    decoded = (inputs.astype(jnp.float32) + up_conv(w_up, deep_out, "co,orw->crw")).astype(
        jnp.bfloat16
    )
    half_r = rows2 // coverage.shape[0]
    half_c = cols2 // coverage.shape[1]
    flags = jnp.repeat(jnp.repeat(coverage, half_r, axis=0), half_c, axis=1).astype(jnp.bfloat16)
    masked = cotangent * flags[None, None, None]
    dy_taps = plane_taps(masked)
    deep_grad = conv_taps(w_up, dy_taps, "co,crw->orw").astype(jnp.bfloat16)
    up_term = jnp.stack(
        [
            jnp.einsum("crw,orw->co", tap, deep_out, preferred_element_type=jnp.float32)
            for tap in dy_taps
        ],
        axis=0,
    )
    dext = margin_ext(deep_grad, steps).astype(jnp.float32)
    hidden_part, kernel_term = dw_backward(dext, kernels, states, start, total2)
    hidden_grad = hidden_part.astype(jnp.bfloat16)
    sig = jax.nn.sigmoid(pre)
    pre_grad = (hidden_grad.astype(jnp.float32) * sig * (1.0 + pre * (1.0 - sig))).astype(
        jnp.bfloat16
    )
    back = up_conv(w_down, pre_grad, "oc,orw->crw")
    grad_input = (masked.astype(jnp.float32) + back).astype(jnp.bfloat16)
    down_term = jnp.stack(
        [
            jnp.einsum("crw,orw->co", tap, pre_grad, preferred_element_type=jnp.float32)
            for tap in in_taps
        ],
        axis=0,
    )
    down, up, small = all_sums(down_term, up_term, kernel_term, scale)
    grad_down = jnp.transpose(down.reshape(9, 64, 128), (0, 2, 1))
    grad_up = up.reshape(9, 64, 128)
    grad_kernels = small[:18].reshape(2, 9, 1)
    return (decoded, grad_input, grad_down, grad_up, grad_kernels)


def solution(mesh):
    placed = (
        P(None, None, None, "lat", "lon"),
        P(),
        P(),
        P(),
        P(None, None, None, "lat", "lon"),
        P("lat", "lon"),
    )
    return jax.shard_map(
        shards,
        mesh=mesh,
        in_specs=placed,
        out_specs=(
            P(None, None, None, "lat", "lon"),
            P(None, None, None, "lat", "lon"),
            P(),
            P(),
            P(None, None, ("lat", "lon")),
        ),
        check_vma=False,
    )
```

```python
import functools
import math

import jax
import jax.numpy as jnp
from jax import lax
from jax.experimental import pallas as pl
from jax.experimental.pallas import tpu as pltpu
from jax.sharding import PartitionSpec as P

BF = jnp.bfloat16
F32 = jnp.float32
ROWS = 24
COLS = 128
CELLS = ROWS * COLS
OFF = 16
WIDE = 160
LO = 8
SPAN = 144
REACH = 136
MESH = pl.DeviceIdType.MESH
N_LAT = 8
N_LON = 16
PIECE = 36
PADDED = 48


def send(src, dst, send_sem, recv_sem, target):
    return pltpu.make_async_remote_copy(
        src_ref=src,
        dst_ref=dst,
        send_sem=send_sem,
        recv_sem=recv_sem,
        device_id=target,
        device_id_type=MESH,
    )


def greet(my_lat, my_lon):
    barrier = pltpu.get_barrier_semaphore()
    peers = [(my_lat, lax.rem(my_lon + d, N_LON)) for d in range(1, N_LON)]
    peers += [(lax.rem(my_lat + d, N_LAT), my_lon) for d in range(1, N_LAT)]
    for down in (1, N_LAT - 1):
        for side in (1, N_LON - 1):
            peers.append((lax.rem(my_lat + down, N_LAT), lax.rem(my_lon + side, N_LON)))
    for peer in peers:
        pl.semaphore_signal(barrier, inc=1, device_id=peer, device_id_type=MESH)
    return barrier, len(peers)


class Sum:
    def __init__(self, my_lat, my_lon, pieces, got, part, parts, whole, sems):
        self.my_lat, self.my_lon = my_lat, my_lon
        self.pieces, self.got, self.part, self.parts, self.whole = pieces, got, part, parts, whole
        self.s1, self.r1, self.s2, self.r2, self.s3, self.r3 = sems

    def lon_peer(self, d):
        return (self.my_lat, lax.rem(self.my_lon + d, N_LON))

    def lat_peer(self, d):
        return (lax.rem(self.my_lat + d, N_LAT), self.my_lon)

    def first(self, d):
        peer = lax.rem(self.my_lon + d, N_LON)
        return send(self.pieces.at[peer], self.got.at[d], self.s1.at[d], self.r1.at[d], self.lon_peer(d))

    def second(self, d):
        return send(self.part, self.parts.at[self.my_lat], self.s2.at[d], self.r2.at[d], self.lat_peer(d))

    def third(self, d):
        mine = self.whole.at[self.my_lon]
        return send(mine, mine, self.s3.at[d], self.r3.at[d], self.lon_peer(d))

    def start_first(self):
        for d in range(1, N_LON):
            self.first(d).start()

    def start_second(self):
        total = self.pieces[self.my_lon].astype(jnp.float32)
        for d in range(1, N_LON):
            self.first(d).wait_recv()
            total = total + self.got[d].astype(jnp.float32)
        rounded = total.astype(jnp.bfloat16)
        self.part[...] = rounded
        self.parts[self.my_lat] = rounded
        for d in range(1, N_LAT):
            self.second(d).start()

    def start_third(self):
        for d in range(1, N_LAT):
            self.second(d).wait_recv()
        total = self.parts[0].astype(jnp.float32)
        for lat in range(1, N_LAT):
            total = total + self.parts[lat].astype(jnp.float32)
        self.whole[self.my_lon] = total.astype(jnp.bfloat16)
        for d in range(1, N_LON):
            self.third(d).start()

    def finish(self, scale, out):
        for d in range(1, N_LON):
            self.third(d).wait_recv()
        for k in range(N_LON):
            piece = self.whole[k].astype(jnp.float32)[:PIECE] * scale
            out[pl.ds(k * PIECE, PIECE), :] = piece
        for d in range(1, N_LON):
            self.first(d).wait_send()
            self.third(d).wait_send()
        for d in range(1, N_LAT):
            self.second(d).wait_send()


class Small(Sum):
    def __init__(self, my_lat, my_lon, mine, got, part, parts, sems):
        self.my_lat, self.my_lon = my_lat, my_lon
        self.mine, self.got, self.part, self.parts = mine, got, part, parts
        self.s1, self.r1, self.s2, self.r2 = sems

    def first(self, d):
        return send(self.mine, self.got.at[d], self.s1.at[d], self.r1.at[d], self.lon_peer(d))

    def start_second(self):
        total = self.mine[...]
        for d in range(1, N_LON):
            self.first(d).wait_recv()
            total = total + self.got[d]
        self.part[...] = total
        for d in range(1, N_LAT):
            self.second(d).start()

    def second(self, d):
        return send(self.part, self.parts.at[d], self.s2.at[d], self.r2.at[d], self.lat_peer(d))

    def finish(self, scale, out):
        total = self.part[...]
        for d in range(1, N_LAT):
            self.second(d).wait_recv()
            total = total + self.parts[d]
        lane = lax.broadcasted_iota(jnp.int32, total.shape, 1)
        mine = lane == self.my_lat * N_LON + self.my_lon
        out[...] = jnp.sum(jnp.where(mine, total, 0.0), axis=1, keepdims=True) * scale
        for d in range(1, N_LON):
            self.first(d).wait_send()
        for d in range(1, N_LAT):
            self.second(d).wait_send()


def sum_scratch():
    return [
        pltpu.VMEM((N_LON, PADDED, 128), jnp.bfloat16),
        pltpu.VMEM((N_LON, PADDED, 128), jnp.bfloat16),
        pltpu.VMEM((PADDED, 128), jnp.bfloat16),
        pltpu.VMEM((N_LAT, PADDED, 128), jnp.bfloat16),
        pltpu.VMEM((N_LON, PADDED, 128), jnp.bfloat16),
    ] + [pltpu.SemaphoreType.DMA((n,)) for n in (N_LON, N_LON, N_LAT, N_LAT, N_LON, N_LON)]


def small_scratch(shape):
    return [
        pltpu.VMEM((N_LON,) + shape, jnp.float32),
        pltpu.VMEM(shape, jnp.float32),
        pltpu.VMEM((N_LAT,) + shape, jnp.float32),
    ] + [pltpu.SemaphoreType.DMA((n,)) for n in (N_LON, N_LON, N_LAT, N_LAT)]


def turned(block):
    eye = (
        lax.broadcasted_iota(jnp.int32, (COLS, COLS), 0)
        == lax.broadcasted_iota(jnp.int32, (COLS, COLS), 1)
    ).astype(BF)
    return lax.dot_general(eye, block, (((1,), (1,)), ((), ())), preferred_element_type=F32)


def row_at(i):
    return pl.ds(pl.multiple_of(i * COLS, COLS), COLS)


def lay_weights(source, target):
    for a in range(3):
        top, mid, end = a * 128, a * 128 + 64, a * 128 + 128
        target[top:mid, 0:128] = source[3 * a + 1]
        target[mid:end, 0:128] = source[3 * a + 2]
        target[top:mid, 128:256] = jnp.zeros((64, 128), BF)
        target[mid:end, 128:256] = source[3 * a]


def loop(low, high, body):
    def step(i, carry):
        body(i)
        return carry

    lax.fori_loop(low, high, step, 0)


def taps_sum(field, row, base, coefs, first, rows_of, cols_of, span):
    acc = field[row, pl.ds(base, span), :]
    for a in range(3):
        for b in range(3):
            coef = coefs[pl.ds(first + 3 * a + b, 1), :]
            acc = acc + coef * field[rows_of(a), pl.ds(cols_of(b), span), :]
    return acc


def kernel(
    scale, x_hbm, c_hbm, cov, wd, wu, kern,
    dec_hbm, gi_hbm, down_out, up_out, small_out,
    xa0, xa1, ma0, ma1, xb0, xb1, mb0, mb1, wdm, wum, yx, ym,
    s0, s1, r2, r1, ds_, d2, pg2, dec, gi, tmp, pack_l, pack_r,
    send_l, send_r, got_l, got_r, got_lc, got_rc, row_x, row_m,
    tile_l, tile_r, e2_up, e2_dn, got_up, got_dn, grad, flat, small_mine,
    in_sem, out_sem, e1_s, e1_r, e2_s, e2_r, e3_s, e3_r, *sums
):
    my_lat, my_lon = lax.axis_index("lat"), lax.axis_index("lon")
    up_lat, dn_lat = lax.rem(my_lat + N_LAT - 1, N_LAT), lax.rem(my_lat + 1, N_LAT)
    lt_lon, rt_lon = lax.rem(my_lon + N_LON - 1, N_LON), lax.rem(my_lon + 1, N_LON)
    has_up = (my_lat > 0).astype(F32)
    has_dn = (my_lat < N_LAT - 1).astype(F32)
    down = Sum(my_lat, my_lon, *sums[:5], sums[5:11])
    up = Sum(my_lat, my_lon, *sums[11:16], sums[16:22])
    small = Small(my_lat, my_lon, small_mine, *sums[22:25], sums[25:29])

    loads = [
        pltpu.make_async_copy(x_hbm.at[0], xa0, in_sem.at[0]),
        pltpu.make_async_copy(x_hbm.at[1], xa1.at[:, pl.ds(COLS, CELLS)], in_sem.at[1]),
        pltpu.make_async_copy(c_hbm.at[0], ma0, in_sem.at[2]),
        pltpu.make_async_copy(c_hbm.at[1], ma1.at[:, pl.ds(COLS, CELLS)], in_sem.at[3]),
    ]
    for load in loads:
        load.start()
    barrier, met = greet(my_lat, my_lon)
    lay_weights(wd, wdm)
    lay_weights(wu, wum)
    spread = (
        lax.broadcasted_iota(jnp.int32, (16, COLS), 0)
        == lax.broadcasted_iota(jnp.int32, (16, COLS), 1) // 8
    ).astype(BF)
    flags = jnp.dot(cov[...].astype(F32).astype(BF), spread, preferred_element_type=F32).astype(BF)
    for load in loads:
        load.wait()

    for q in range(3):
        flag = flags[q : q + 1, :]

        def turn(i, flag=flag):
            here, after = row_at(i), row_at(i + 1)
            ma0[:, here] = ma0[:, here] * flag
            ma1[:, after] = ma1[:, after] * flag
            for u, (field, at, into, shift) in enumerate(
                (
                    (xa0, here, xb0, here),
                    (xa1, after, xb1, after),
                    (ma0, here, mb0, here),
                    (ma1, after, mb1, after),
                )
            ):
                block = turned(field[:, at])
                into[shift, :] = block.astype(BF)
                spot = (u % 2) * 192 + i * 8 + (u // 2) * 4
                pack_l[pl.ds(spot, 4), :] = block[0:4]
                pack_r[pl.ds(spot, 4), :] = block[COLS - 4 : COLS]

        loop(8 * q, 8 * q + 8, turn)
    send_l[...] = pack_l[...].astype(BF)
    send_r[...] = pack_r[...].astype(BF)

    pl.semaphore_wait(barrier, met)
    last = pl.ds(ROWS * COLS, COLS)
    corner = pl.ds(368, 16)
    first = [
        send(send_l, got_r, e1_s.at[0], e1_r.at[0], (my_lat, lt_lon)),
        send(send_r, got_l, e1_s.at[1], e1_r.at[1], (my_lat, rt_lon)),
        send(send_l.at[corner], got_rc, e1_s.at[2], e1_r.at[2], (dn_lat, lt_lon)),
        send(send_r.at[corner], got_lc, e1_s.at[3], e1_r.at[3], (dn_lat, rt_lon)),
        send(xa1.at[:, last], row_x, e1_s.at[4], e1_r.at[4], (dn_lat, my_lon)),
        send(ma1.at[:, last], row_m, e1_s.at[5], e1_r.at[5], (dn_lat, my_lon)),
    ]
    for copy in first:
        copy.start()

    def conv_row(i):
        here, after = row_at(i), row_at(i + 1)
        for b0, b1, weight, y in ((xb0, xb1, wdm, yx), (mb0, mb1, wum, ym)):
            taps = jnp.concatenate([b1[here, :], b0[here, :], b1[after, :]], axis=1)
            y[i, OFF : OFF + COLS, :] = jnp.dot(taps, weight[...], preferred_element_type=F32)

    loop(1, ROWS, conv_row)

    for copy in first:
        copy.wait_recv()
    for got, field, into in ((row_x, xa1, xb1), (row_m, ma1, mb1)):
        row = got[...] * has_up.astype(BF)
        field[:, 0:COLS] = row
        into[0:COLS, :] = turned(row).astype(BF)
    conv_row(0)
    for got, edge, tile, at in ((got_l, got_lc, tile_l, 12), (got_r, got_rc, tile_r, 144)):
        tile[0:8, :] = edge[...].astype(F32)[8:16] * has_up
        tile[8:200, :] = got[192:384, :].astype(F32)
        taps = jnp.concatenate(
            [tile[0:192, :].astype(BF), got[0:192, :], tile[8:200, :].astype(BF)], axis=1
        )
        for weight, y, part in ((wdm, yx, 0), (wum, ym, 4)):
            rim = jnp.dot(taps, weight[...], preferred_element_type=F32)
            for i in range(ROWS):
                y[i, at : at + 4, :] = rim[i * 8 + part : i * 8 + part + 4]

    def activate(i):
        span, before = pl.ds(LO, SPAN), pl.ds(LO - 1, SPAN)
        pre = yx[i, span, 0:128] + yx[i, before, 128:256]
        sig = 0.5 * jnp.tanh(0.5 * pre) + 0.5
        s0[i + 2, span, :] = (pre * sig).astype(BF).astype(F32)
        ds_[i, span, :] = sig * (1.0 + pre * (1.0 - sig))
        grad_row = ym[i, span, 0:128] + ym[i, before, 128:256]
        r2[i + 2, span, :] = grad_row.astype(BF).astype(F32)

    for i in (0, 1, ROWS - 2, ROWS - 1):
        activate(i)
    for n, field in enumerate((s0, r2)):
        for k in range(2):
            at = pl.ds(n * 288 + k * SPAN, SPAN)
            e2_up[at, :] = field[2 + k, LO : LO + SPAN, :].astype(BF)
            e2_dn[at, :] = field[ROWS + k, LO : LO + SPAN, :].astype(BF)
    second = [
        send(e2_up, got_up, e2_s.at[0], e2_r.at[0], (up_lat, my_lon)),
        send(e2_dn, got_dn, e2_s.at[1], e2_r.at[1], (dn_lat, my_lon)),
    ]
    for copy in second:
        copy.start()
    loop(2, ROWS - 2, activate)

    def forward_1(r):
        acc = taps_sum(s0, r + 1, LO, kern, 0, lambda a: r + a, lambda b: LO - 1 + b, SPAN)
        s1[r, pl.ds(LO, SPAN), :] = acc

    def backward_1(r):
        acc = taps_sum(r2, r + 1, LO, kern, 9, lambda a: r - a + 2, lambda b: LO + 1 - b, SPAN)
        r1[r, pl.ds(LO, SPAN), :] = acc

    loop(2, ROWS, forward_1)
    loop(2, ROWS, backward_1)
    for copy in second:
        copy.wait_recv()
    for n, field in enumerate((s0, r2)):
        for k in range(2):
            at = pl.ds(n * 288 + k * SPAN, SPAN)
            field[k, LO : LO + SPAN, :] = got_dn[at, :].astype(F32) * has_up
            field[ROWS + 2 + k, LO : LO + SPAN, :] = got_up[at, :].astype(F32) * has_dn
    for r in (0, 1, ROWS, ROWS + 1):
        forward_1(r)
        backward_1(r)
    for field in (s1, r1):
        field[0, LO : LO + SPAN, :] = field[0, LO : LO + SPAN, :] * has_up
        field[ROWS + 1, LO : LO + SPAN, :] = field[ROWS + 1, LO : LO + SPAN, :] * has_dn

    def pair(value, slot, into, i):
        tmp[slot, 0:REACH, :] = value
        here = row_at(i)
        into[here, 0:128] = tmp[slot, 0:COLS, :].astype(BF)
        into[here, 128:256] = tmp[slot, 1 : COLS + 1, :].astype(BF)

    def backward_0(i):
        acc = taps_sum(r1, i + 1, OFF, kern, 0, lambda a: i - a + 2, lambda b: OFF + 1 - b, REACH)
        value = acc.astype(BF).astype(F32) * ds_[i, pl.ds(OFF, REACH), :]
        pair(value, 0, pg2, i)

    loop(0, ROWS, backward_0)
    third = [
        send(pg2.at[pl.ds(0, COLS)], pg2.at[pl.ds(CELLS, COLS)], e3_s.at[0], e3_r.at[0], (up_lat, my_lon)),
        send(d2.at[pl.ds(0, COLS)], d2.at[pl.ds(CELLS, COLS)], e3_s.at[1], e3_r.at[1], (up_lat, my_lon)),
    ]
    third[0].start()

    def weight_grad(a0, a1, pairs, total):
        grad[...] = jnp.zeros_like(grad)

        def step(n):
            at = pl.ds(pl.multiple_of(n * 512, 512), 512)
            after = pl.ds(pl.multiple_of(n * 512 + COLS, COLS), 512)
            taps = jnp.concatenate([a1[:, at], a0[:, at], a1[:, after]], axis=0)
            grad[...] += jnp.dot(taps, pairs[at, :], preferred_element_type=F32)

        loop(0, ROWS // 4, step)
        for a in range(3):
            top, mid, end = a * 128, a * 128 + 64, a * 128 + 128
            flat[(3 * a + 1) * 64 : (3 * a + 2) * 64, :] = grad[top:mid, 0:128]
            flat[(3 * a + 2) * 64 : (3 * a + 3) * 64, :] = grad[mid:end, 0:128]
            flat[3 * a * 64 : (3 * a + 1) * 64, :] = grad[mid:end, 128:256]
        for k in range(N_LON):
            total.pieces[k] = flat[pl.ds(k * PIECE, PADDED), :].astype(BF)
        total.start_first()

    flat[576:624, :] = jnp.zeros((48, 128), F32)
    weight_grad(xa0, xa1, pg2, down)

    def forward_0(i):
        acc = taps_sum(s1, i + 1, OFF, kern, 9, lambda a: i + a, lambda b: OFF - 1 + b, REACH)
        pair(acc, 1, d2, i)

    loop(0, ROWS, forward_0)
    third[1].start()
    weight_grad(ma0, ma1, d2, up)

    def kernel_grad(left, left_row, right, right_row, first_row):
        def step(i, accs):
            own = left[i + left_row, OFF : OFF + COLS, :]
            found = []
            for a in range(3):
                for b in range(3):
                    other = right[i + a + right_row, pl.ds(OFF - 1 + b, COLS), :]
                    found.append(accs[3 * a + b] + jnp.sum((own * other).reshape(16, 8, 128), axis=0))
            return tuple(found)

        accs = lax.fori_loop(0, ROWS, step, tuple(jnp.zeros((8, 128), F32) for _ in range(9)))
        for t in range(9):
            small_mine[first_row + t : first_row + t + 1, :] = jnp.sum(accs[t], axis=0, keepdims=True)

    small_mine[16:24, :] = jnp.zeros((8, 128), F32)
    kernel_grad(r1, 1, s0, 1, 0)
    kernel_grad(r2, 2, s1, 0, 9)
    small.start_first()

    down.start_second()

    def add_conv(weight, pairs, f0, f1, out):
        def step(n):
            at = pl.ds(pl.multiple_of(n * 512, 512), 512)
            after = pl.ds(pl.multiple_of(n * 512 + COLS, COLS), 512)
            nt = (((1,), (1,)), ((), ()))
            here, below = pairs[at, :], pairs[after, :]
            even = lax.dot_general(weight[128:256, :], here, nt, preferred_element_type=F32)
            odd = lax.dot_general(weight[256:384, :], here, nt, preferred_element_type=F32)
            odd = odd + lax.dot_general(weight[0:128, :], below, nt, preferred_element_type=F32)
            out[0, :, at] = (f0[:, at].astype(F32) + even).astype(BF)
            out[1, :, at] = (f1[:, after].astype(F32) + odd).astype(BF)

        loop(0, ROWS // 4, step)

    below = pl.ds(CELLS, COLS)
    third[1].wait_recv()
    d2[below, :] = d2[below, :] * has_dn.astype(BF)
    add_conv(wum, d2, xa0, xa1, dec)
    store_dec = pltpu.make_async_copy(dec, dec_hbm, out_sem.at[0])
    store_dec.start()
    up.start_second()
    down.start_third()
    small.start_second()
    third[0].wait_recv()
    pg2[below, :] = pg2[below, :] * has_dn.astype(BF)
    add_conv(wdm, pg2, ma0, ma1, gi)
    store_gi = pltpu.make_async_copy(gi, gi_hbm, out_sem.at[1])
    store_gi.start()
    up.start_third()
    down.finish(scale, down_out)
    small.finish(scale, small_out)
    up.finish(scale, up_out)
    for copy in first + second + third:
        copy.wait_send()
    store_dec.wait()
    store_gi.wait()


def level(x, c, cov, wd, wu, kern, scale):
    vmem = pl.BlockSpec(memory_space=pltpu.VMEM)
    hbm = pl.BlockSpec(memory_space=pl.ANY)
    wide = lambda rows: pltpu.VMEM((rows, WIDE, 128), F32)
    mat = lambda rows, cols=128: pltpu.VMEM((rows, cols), BF)
    dma = lambda n: pltpu.SemaphoreType.DMA((n,))
    tall = (ROWS + 1) * COLS
    planes = jax.ShapeDtypeStruct((2, 128, CELLS), BF)
    scratch = (
        [mat(128, CELLS), mat(128, tall)] * 2
        + [mat(CELLS), mat(tall)] * 2
        + [mat(384, 256)] * 2
        + [pltpu.VMEM((ROWS, WIDE, 256), F32)] * 2
        + [wide(ROWS + 4), wide(ROWS + 2), wide(ROWS + 4), wide(ROWS + 2), wide(ROWS)]
        + [mat(tall, 256)] * 2
        + [pltpu.VMEM((2, 128, CELLS), BF)] * 2
        + [pltpu.VMEM((2, REACH, 128), F32)]
        + [pltpu.VMEM((384, 128), F32)] * 2
        + [mat(384)] * 4
        + [mat(16)] * 2
        + [mat(128)] * 2
        + [pltpu.VMEM((200, 128), F32)] * 2
        + [mat(576)] * 4
        + [pltpu.VMEM((384, 256), F32), pltpu.VMEM((624, 128), F32), pltpu.VMEM((24, 128), F32)]
        + [dma(4), dma(2), dma(6), dma(6), dma(2), dma(2), dma(2), dma(2)]
        + sum_scratch()
        + sum_scratch()
        + small_scratch((24, 128))
    )
    return pl.pallas_call(
        functools.partial(kernel, scale),
        out_shape=(
            planes,
            planes,
            jax.ShapeDtypeStruct((576, 128), F32),
            jax.ShapeDtypeStruct((576, 128), F32),
            jax.ShapeDtypeStruct((24, 1), F32),
        ),
        in_specs=[hbm, hbm, vmem, vmem, vmem, vmem],
        out_specs=(hbm, hbm, vmem, vmem, vmem),
        scratch_shapes=scratch,
        compiler_params=pltpu.CompilerParams(
            collective_id=0, has_side_effects=True, vmem_limit_bytes=56 * 1024 * 1024
        ),
        cost_estimate=pl.CostEstimate(flops=3_600_000_000, bytes_accessed=7_000_000, transcendentals=500_000),
    )(x, c, cov, wd, wu, kern)


def shards(inputs, kernels, w_down, w_up, cotangent, coverage):
    total = inputs.shape[3] * inputs.shape[4] * N_LAT * N_LON
    scale = 1.0 / math.sqrt(total)

    def gathered(planes):
        return jnp.transpose(planes, (1, 2, 0, 3, 4)).reshape(2, 128, CELLS)

    def spread(planes):
        return jnp.transpose(planes.reshape(2, 2, 64, ROWS, COLS), (2, 0, 1, 3, 4))

    decoded, grad_input, down, up, small = level(
        gathered(inputs),
        gathered(cotangent),
        coverage,
        jnp.transpose(w_down, (0, 2, 1)),
        w_up,
        kernels.reshape(18, 128),
        scale,
    )
    return (
        spread(decoded),
        spread(grad_input),
        jnp.transpose(down.reshape(9, 64, 128), (0, 2, 1)),
        up.reshape(9, 64, 128),
        small[:18].reshape(2, 9, 1),
    )


def solution(mesh):
    placed = (
        P(None, None, None, "lat", "lon"),
        P(),
        P(),
        P(),
        P(None, None, None, "lat", "lon"),
        P("lat", "lon"),
    )
    return jax.shard_map(
        shards,
        mesh=mesh,
        in_specs=placed,
        out_specs=(
            P(None, None, None, "lat", "lon"),
            P(None, None, None, "lat", "lon"),
            P(),
            P(),
            P(None, None, ("lat", "lon")),
        ),
        check_vma=False,
    )
```

```python
import functools
import math

import jax
import jax.numpy as jnp
from jax import lax
from jax.experimental import pallas as pl
from jax.experimental.pallas import tpu as pltpu
from jax.sharding import PartitionSpec as P

BF = jnp.bfloat16
F32 = jnp.float32
ROWS = 24
COLS = 128
CELLS = ROWS * COLS
OFF = 16
WIDE = 160
LO = 8
SPAN = 144
REACH = 136
MESH = pl.DeviceIdType.MESH
N_LAT = 8
N_LON = 16
PIECE = 36
PADDED = 48


def send(src, dst, send_sem, recv_sem, target):
    return pltpu.make_async_remote_copy(
        src_ref=src,
        dst_ref=dst,
        send_sem=send_sem,
        recv_sem=recv_sem,
        device_id=target,
        device_id_type=MESH,
    )


def greet(my_lat, my_lon):
    barrier = pltpu.get_barrier_semaphore()
    peers = [(my_lat, lax.rem(my_lon + d, N_LON)) for d in range(1, N_LON)]
    peers += [(lax.rem(my_lat + d, N_LAT), my_lon) for d in range(1, N_LAT)]
    for down in (1, N_LAT - 1):
        for side in (1, N_LON - 1):
            peers.append((lax.rem(my_lat + down, N_LAT), lax.rem(my_lon + side, N_LON)))
    for peer in peers:
        pl.semaphore_signal(barrier, inc=1, device_id=peer, device_id_type=MESH)
    return barrier, len(peers)


class Sum:
    def __init__(self, my_lat, my_lon, pieces, got, part, parts, whole, *sems):
        self.my_lat, self.my_lon = my_lat, my_lon
        self.pieces, self.got, self.part, self.parts, self.whole = pieces, got, part, parts, whole
        self.s1, self.r1, self.s2, self.r2, self.s3, self.r3 = sems

    def lon_peer(self, d):
        return (self.my_lat, lax.rem(self.my_lon + d, N_LON))

    def lat_peer(self, d):
        return (lax.rem(self.my_lat + d, N_LAT), self.my_lon)

    def first(self, d):
        peer = lax.rem(self.my_lon + d, N_LON)
        return send(self.pieces.at[peer], self.got.at[d], self.s1, self.r1, self.lon_peer(d))

    def second(self, d):
        return send(self.part, self.parts.at[d], self.s2, self.r2, self.lat_peer(d))

    def third(self, d):
        return send(self.part, self.whole.at[d], self.s3, self.r3, self.lon_peer(d))

    def all_of(self, buffer, sent, received):
        arrived = buffer.at[pl.ds(1, buffer.shape[0] - 1)]
        return send(arrived, arrived, sent, received, self.lon_peer(1))

    def start_first(self):
        for d in range(1, N_LON):
            self.first(d).start()

    def start_second(self):
        self.all_of(self.got, self.s1, self.r1).wait_recv()
        total = self.pieces[self.my_lon].astype(jnp.float32)
        for d in range(1, N_LON):
            total = total + self.got[d].astype(jnp.float32)
        rounded = total.astype(jnp.bfloat16)
        self.part[...] = rounded
        self.parts[0] = rounded
        for d in range(1, N_LAT):
            self.second(d).start()

    def start_third(self):
        self.all_of(self.parts, self.s2, self.r2).wait()
        total = jnp.zeros((PADDED, 128), jnp.float32)
        for lat in range(N_LAT):
            slot = lax.rem(self.my_lat - lat + N_LAT, N_LAT)
            total = total + self.parts[slot].astype(jnp.float32)
        rounded = total.astype(jnp.bfloat16)
        self.part[...] = rounded
        self.whole[0] = rounded
        for d in range(1, N_LON):
            self.third(d).start()

    def finish(self, scale, out):
        self.all_of(self.whole, self.s3, self.r3).wait_recv()
        for d in range(N_LON):
            k = lax.rem(self.my_lon - d + N_LON, N_LON)
            piece = self.whole[d].astype(jnp.float32)[:PIECE] * scale
            out[pl.ds(k * PIECE, PIECE), :] = piece

    def settle(self):
        self.all_of(self.got, self.s1, self.r1).wait_send()
        self.all_of(self.whole, self.s3, self.r3).wait_send()


class Small(Sum):
    def __init__(self, my_lat, my_lon, mine, got, part, parts, *sems):
        self.my_lat, self.my_lon = my_lat, my_lon
        self.mine, self.got, self.part, self.parts = mine, got, part, parts
        self.s1, self.r1, self.s2, self.r2 = sems

    def first(self, d):
        return send(self.mine, self.got.at[d], self.s1, self.r1, self.lon_peer(d))

    def start_second(self):
        self.all_of(self.got, self.s1, self.r1).wait_recv()
        total = self.mine[...]
        for d in range(1, N_LON):
            total = total + self.got[d]
        self.part[...] = total
        for d in range(1, N_LAT):
            self.second(d).start()

    def finish(self, scale, out):
        self.all_of(self.parts, self.s2, self.r2).wait_recv()
        total = self.part[...]
        for d in range(1, N_LAT):
            total = total + self.parts[d]
        lane = lax.broadcasted_iota(jnp.int32, total.shape, 1)
        mine = lane == self.my_lat * N_LON + self.my_lon
        column = jnp.sum(jnp.where(mine, total, 0.0), axis=1, keepdims=True) * scale
        row = lax.broadcasted_iota(jnp.int32, total.shape, 0)
        for t in range(2):
            line = jnp.sum(jnp.where(row == lane + 9 * t, column, 0.0), axis=0, keepdims=True)
            out[t] = line[:, 0:9]

    def settle(self):
        self.all_of(self.got, self.s1, self.r1).wait_send()
        self.all_of(self.parts, self.s2, self.r2).wait_send()


def sum_scratch():
    return [
        pltpu.VMEM((N_LON, PADDED, 128), jnp.bfloat16),
        pltpu.VMEM((N_LON, PADDED, 128), jnp.bfloat16),
        pltpu.VMEM((PADDED, 128), jnp.bfloat16),
        pltpu.VMEM((N_LAT, PADDED, 128), jnp.bfloat16),
        pltpu.VMEM((N_LON, PADDED, 128), jnp.bfloat16),
    ] + [pltpu.SemaphoreType.DMA] * 6


def small_scratch(shape):
    return [
        pltpu.VMEM((N_LON,) + shape, jnp.float32),
        pltpu.VMEM(shape, jnp.float32),
        pltpu.VMEM((N_LAT,) + shape, jnp.float32),
    ] + [pltpu.SemaphoreType.DMA] * 4


def row_at(i):
    return pl.ds(pl.multiple_of(i * COLS, COLS), COLS)


def lay_weights(source, target):
    for a in range(3):
        top, mid, end = a * 128, a * 128 + 64, a * 128 + 128
        target[top:mid, 0:128] = source[3 * a + 1]
        target[mid:end, 0:128] = source[3 * a + 2]
        target[top:mid, 128:256] = jnp.zeros((64, 128), BF)
        target[mid:end, 128:256] = source[3 * a]


def loop(low, high, body, wide=1):
    def step(n, carry):
        for k in range(wide):
            body(low + n * wide + k)
        return carry

    lax.fori_loop(0, (high - low) // wide, step, 0)


def plane_rows(i):
    return pl.ds(i, 64, stride=ROWS)


def taps_sum(field, row, base, coefs, first, rows_of, cols_of, span):
    acc = field[row, pl.ds(base, span), :]
    for a in range(3):
        for b in range(3):
            coef = coefs[3 * a + b, first : first + 1, :]
            acc = acc + coef * field[rows_of(a), pl.ds(cols_of(b), span), :]
    return acc


def kernel(
    scale, x_hbm, c_hbm, cov_hbm, wd_hbm, wu_hbm, kern_hbm,
    dec_hbm, gi_hbm, down_hbm, up_hbm, small_hbm,
    xa0, xa1, ma0, ma1, xb0, xb1, mb0, mb1, wdm, wum, yx, ym,
    s0, s1, r2, r1, ds_, d2, pg2, tmp, pack_l, pack_r,
    down_out, up_out, small_out, cov, wd, wu, kern, raw_x, raw_c, planes_x, planes_c, send_l, send_r, got_l, got_r, got_lc, got_rc, row_x, row_m,
    tile_l, tile_r, e2_up, e2_dn, got_up, got_dn, grad, flat, small_mine,
    in_sem, out_sem, e1_s, e1_r, e2_s, e2_r, e3_s, e3_r, *sums
):
    my_lat, my_lon = lax.axis_index("lat"), lax.axis_index("lon")
    up_lat, dn_lat = lax.rem(my_lat + N_LAT - 1, N_LAT), lax.rem(my_lat + 1, N_LAT)
    lt_lon, rt_lon = lax.rem(my_lon + N_LON - 1, N_LON), lax.rem(my_lon + 1, N_LON)
    has_up = (my_lat > 0).astype(F32)
    has_dn = (my_lat < N_LAT - 1).astype(F32)
    down = Sum(my_lat, my_lon, *sums[:11])
    up = Sum(my_lat, my_lon, *sums[11:22])
    small = Small(my_lat, my_lon, small_mine, *sums[22:29])

    loads = []
    for n, (source, raw) in enumerate(((x_hbm, raw_x), (c_hbm, raw_c))):
        for u in range(2):
            for v in range(2):
                p = 2 * u + v
                loads.append(
                    pltpu.make_async_copy(source.at[:, u, v], raw.at[p], in_sem.at[4 * n + p])
                )
    params = [
        pltpu.make_async_copy(source, target, in_sem.at[8 + n])
        for n, (source, target) in enumerate(
            ((cov_hbm, cov), (wd_hbm, wd), (wu_hbm, wu), (kern_hbm, kern))
        )
    ]
    for load in params + loads:
        load.start()
    barrier, met = greet(my_lat, my_lon)
    for load in params:
        load.wait()
    lay_weights(wd, wdm)
    lay_weights(wu, wum)
    spread = (
        lax.broadcasted_iota(jnp.int32, (16, COLS), 0)
        == lax.broadcasted_iota(jnp.int32, (16, COLS), 1) // 8
    ).astype(BF)
    flags = jnp.dot(cov[...].astype(F32).astype(BF), spread, preferred_element_type=F32).astype(BF)

    def unfold(raw, planes, p):
        def step(g):
            block = raw[p, pl.ds(g * 16, 16)].astype(F32)
            planes[p, pl.ds(pl.multiple_of(g * 384, 384), 384), :] = block.reshape(384, COLS)

        loop(0, 4, step)

    def turn(u, flag, planes, field, into, part, i):
        at = row_at(i + u)
        block = jnp.concatenate(
            [planes[2 * u, plane_rows(i), :], planes[2 * u + 1, plane_rows(i), :]], axis=0
        ).astype(BF)
        if flag is not None:
            block = block * flag
        field[:, at] = block
        block = block.T
        into[at, :] = block
        block = block.astype(F32)
        spot = u * 192 + i * 8 + part
        pack_l[pl.ds(spot, 4), :] = block[0:4]
        pack_r[pl.ds(spot, 4), :] = block[COLS - 4 : COLS]

    for u, field, into in ((0, xa0, xb0), (1, xa1, xb1)):
        for v in range(2):
            loads[2 * u + v].wait()
            unfold(raw_x, planes_x, 2 * u + v)
        loop(0, ROWS, functools.partial(turn, u, None, planes_x, field, into, 0), 4)
    for u, field, into in ((0, ma0, mb0), (1, ma1, mb1)):
        for v in range(2):
            loads[4 + 2 * u + v].wait()
            unfold(raw_c, planes_c, 2 * u + v)
        for q in range(3):
            body = functools.partial(turn, u, flags[q : q + 1, :], planes_c, field, into, 4)
            loop(8 * q, 8 * q + 8, body, 4)
    send_l[...] = pack_l[...].astype(BF)
    send_r[...] = pack_r[...].astype(BF)

    pl.semaphore_wait(barrier, met)
    last = pl.ds(ROWS * COLS, COLS)
    corner = pl.ds(368, 16)
    first = [
        send(send_l, got_r, e1_s.at[0], e1_r.at[0], (my_lat, lt_lon)),
        send(send_r, got_l, e1_s.at[1], e1_r.at[1], (my_lat, rt_lon)),
        send(send_l.at[corner], got_rc, e1_s.at[2], e1_r.at[2], (dn_lat, lt_lon)),
        send(send_r.at[corner], got_lc, e1_s.at[3], e1_r.at[3], (dn_lat, rt_lon)),
        send(xa1.at[:, last], row_x, e1_s.at[4], e1_r.at[4], (dn_lat, my_lon)),
        send(ma1.at[:, last], row_m, e1_s.at[5], e1_r.at[5], (dn_lat, my_lon)),
    ]
    for copy in first:
        copy.start()

    def conv_rows(i, count):
        here = pl.ds(pl.multiple_of(i * COLS, COLS), count * COLS)
        after = pl.ds(pl.multiple_of((i + 1) * COLS, COLS), count * COLS)
        for b0, b1, weight, y in ((xb0, xb1, wdm, yx), (mb0, mb1, wum, ym)):
            taps = jnp.concatenate([b1[here, :], b0[here, :], b1[after, :]], axis=1)
            found = jnp.dot(taps, weight[...], preferred_element_type=F32)
            for k in range(count):
                y[i + k, OFF : OFF + COLS, :] = found[k * COLS : (k + 1) * COLS]

    conv_rows(1, 3)
    loop(1, ROWS // 4, lambda n: conv_rows(4 * n, 4))

    def activate(i, low=LO, count=SPAN):
        span, before = pl.ds(low, count), pl.ds(low - 1, count)
        pre = yx[i, span, 0:128] + yx[i, before, 128:256]
        sig = 0.5 * jnp.tanh(0.5 * pre) + 0.5
        s0[i + 2, span, :] = (pre * sig).astype(BF).astype(F32)
        ds_[i, span, :] = sig * (1.0 + pre * (1.0 - sig))
        grad_row = ym[i, span, 0:128] + ym[i, before, 128:256]
        r2[i + 2, span, :] = grad_row.astype(BF).astype(F32)

    def rims(i):
        activate(i, LO, 16)
        activate(i, OFF + COLS, 8)

    loop(1, ROWS - 1, activate, 2)
    activate(ROWS - 1)

    for copy in first:
        copy.wait_recv()
    for got, field, into in ((row_x, xa1, xb1), (row_m, ma1, mb1)):
        row = got[...] * has_up.astype(BF)
        field[:, 0:COLS] = row
        into[0:COLS, :] = row.T
    conv_rows(0, 1)
    for got, edge, tile, at in ((got_l, got_lc, tile_l, 12), (got_r, got_rc, tile_r, 144)):
        tile[0:8, :] = edge[...].astype(F32)[8:16] * has_up
        tile[8:200, :] = got[192:384, :].astype(F32)
        taps = jnp.concatenate(
            [tile[0:192, :].astype(BF), got[0:192, :], tile[8:200, :].astype(BF)], axis=1
        )
        for weight, y, part in ((wdm, yx, 0), (wum, ym, 4)):
            rim = jnp.dot(taps, weight[...], preferred_element_type=F32)
            for i in range(ROWS):
                y[i, at : at + 4, :] = rim[i * 8 + part : i * 8 + part + 4]

    for i in (0, 1, ROWS - 2, ROWS - 1):
        rims(i) if i else activate(i)
    for n, field in enumerate((s0, r2)):
        for k in range(2):
            at = pl.ds(n * 288 + k * SPAN, SPAN)
            e2_up[at, :] = field[2 + k, LO : LO + SPAN, :].astype(BF)
            e2_dn[at, :] = field[ROWS + k, LO : LO + SPAN, :].astype(BF)
    second = [
        send(e2_up, got_up, e2_s.at[0], e2_r.at[0], (up_lat, my_lon)),
        send(e2_dn, got_dn, e2_s.at[1], e2_r.at[1], (dn_lat, my_lon)),
    ]
    for copy in second:
        copy.start()
    loop(2, ROWS - 2, rims, 4)

    def forward_1(r):
        acc = taps_sum(s0, r + 1, LO, kern, 0, lambda a: r + a, lambda b: LO - 1 + b, SPAN)
        s1[r, pl.ds(LO, SPAN), :] = acc

    def backward_1(r):
        acc = taps_sum(r2, r + 1, LO, kern, 1, lambda a: r - a + 2, lambda b: LO + 1 - b, SPAN)
        r1[r, pl.ds(LO, SPAN), :] = acc

    loop(2, ROWS, forward_1, 2)
    loop(2, ROWS, backward_1, 2)
    def pair(value, slot, into, i):
        slot = slot + lax.rem(i, 2)
        tmp[slot, 0:REACH, :] = value
        here = row_at(i)
        into[here, 0:128] = tmp[slot, 0:COLS, :].astype(BF)
        into[here, 128:256] = tmp[slot, 1 : COLS + 1, :].astype(BF)

    def backward_0(i):
        acc = taps_sum(r1, i + 1, OFF, kern, 0, lambda a: i - a + 2, lambda b: OFF + 1 - b, REACH)
        value = acc.astype(BF).astype(F32) * ds_[i, pl.ds(OFF, REACH), :]
        pair(value, 0, pg2, i)

    def forward_0(i):
        acc = taps_sum(s1, i + 1, OFF, kern, 1, lambda a: i + a, lambda b: OFF - 1 + b, REACH)
        pair(acc, 2, d2, i)

    loop(2, ROWS - 2, backward_0, 2)
    loop(2, ROWS - 2, forward_0, 2)
    for copy in second:
        copy.wait_recv()
    for n, field in enumerate((s0, r2)):
        for k in range(2):
            at = pl.ds(n * 288 + k * SPAN, SPAN)
            field[k, LO : LO + SPAN, :] = got_dn[at, :].astype(F32) * has_up
            field[ROWS + 2 + k, LO : LO + SPAN, :] = got_up[at, :].astype(F32) * has_dn
    for r in (0, 1, ROWS, ROWS + 1):
        forward_1(r)
        backward_1(r)
    for field in (s1, r1):
        field[0, LO : LO + SPAN, :] = field[0, LO : LO + SPAN, :] * has_up
        field[ROWS + 1, LO : LO + SPAN, :] = field[ROWS + 1, LO : LO + SPAN, :] * has_dn

    for i in (0, 1, ROWS - 2, ROWS - 1):
        backward_0(i)
        forward_0(i)
    third = [
        send(pg2.at[pl.ds(0, COLS)], pg2.at[pl.ds(CELLS, COLS)], e3_s.at[0], e3_r.at[0], (up_lat, my_lon)),
        send(d2.at[pl.ds(0, COLS)], d2.at[pl.ds(CELLS, COLS)], e3_s.at[1], e3_r.at[1], (up_lat, my_lon)),
    ]
    for copy in third:
        copy.start()

    def weight_grad(a0, a1, pairs, total):
        half = CELLS // 2
        for n in range(2):
            at, after = pl.ds(n * half, half), pl.ds(n * half + COLS, half)
            taps = jnp.concatenate([a1[:, at], a0[:, at], a1[:, after]], axis=0)
            part = jnp.dot(taps, pairs[at, :], preferred_element_type=F32)
            grad[...] = part if n == 0 else grad[...] + part
        for a in range(3):
            top, mid, end = a * 128, a * 128 + 64, a * 128 + 128
            flat[(3 * a + 1) * 64 : (3 * a + 2) * 64, :] = grad[top:mid, 0:128]
            flat[(3 * a + 2) * 64 : (3 * a + 3) * 64, :] = grad[mid:end, 0:128]
            flat[3 * a * 64 : (3 * a + 1) * 64, :] = grad[mid:end, 128:256]
        for k in range(N_LON):
            total.pieces[k] = flat[pl.ds(k * PIECE, PADDED), :].astype(BF)
        total.start_first()

    flat[576:624, :] = jnp.zeros((48, 128), F32)
    weight_grad(xa0, xa1, pg2, down)

    weight_grad(ma0, ma1, d2, up)

    def kernel_grad(left, left_row, right, right_row, first_row):
        def step(i, accs):
            own = left[i + left_row, OFF : OFF + COLS, :]
            found = []
            for a in range(3):
                for b in range(3):
                    other = right[i + a + right_row, pl.ds(OFF - 1 + b, COLS), :]
                    found.append(accs[3 * a + b] + jnp.sum((own * other).reshape(16, 8, 128), axis=0))
            return tuple(found)

        accs = lax.fori_loop(0, ROWS, step, tuple(jnp.zeros((8, 128), F32) for _ in range(9)))
        for t in range(9):
            small_mine[first_row + t : first_row + t + 1, :] = jnp.sum(accs[t], axis=0, keepdims=True)

    small_mine[16:24, :] = jnp.zeros((8, 128), F32)
    kernel_grad(r1, 1, s0, 1, 0)
    kernel_grad(r2, 2, s1, 0, 9)
    small.start_first()

    def add_piece(weight, pairs, f0, f1, planes, n):
        at = pl.ds(pl.multiple_of(n * 512, 512), 512)
        after = pl.ds(pl.multiple_of(n * 512 + COLS, COLS), 512)
        lines = jnp.concatenate([pairs[row_at(4 * n + k), :].T for k in range(5)], axis=1)
        found = jnp.dot(weight[128:384, :], lines[:, 0:512], preferred_element_type=F32)
        under = jnp.dot(weight[0:128, :], lines[:, COLS:640], preferred_element_type=F32)
        even = f0[:, at].astype(F32) + found[0:128]
        odd = f1[:, after].astype(F32) + found[128:256] + under
        for u, value in ((0, even), (1, odd)):
            for k in range(4):
                for v in range(2):
                    planes[2 * u + v, plane_rows(4 * n + k), :] = value[
                        v * 64 : (v + 1) * 64, k * COLS : (k + 1) * COLS
                    ]

    def put_out(planes, raw, out, sem):
        stores = []
        for u in range(2):
            for v in range(2):
                p = 2 * u + v

                def fold(g, p=p):
                    block = planes[p, pl.ds(pl.multiple_of(g * 384, 384), 384), :]
                    raw[p, pl.ds(g * 16, 16)] = block.astype(BF).reshape(16, ROWS, COLS)

                loop(0, 4, fold)
                stores.append(pltpu.make_async_copy(raw.at[p], out.at[:, u, v], sem.at[p]))
                stores[-1].start()
        return stores

    dec_piece = functools.partial(add_piece, wum, d2, xa0, xa1, planes_x)
    gi_piece = functools.partial(add_piece, wdm, pg2, ma0, ma1, planes_c)
    below = pl.ds(CELLS, COLS)

    loop(0, 3, dec_piece)
    down.start_second()
    for copy, field in zip(third, (pg2, d2)):
        copy.wait_recv()
        field[below, :] = field[below, :] * has_dn.astype(BF)
    loop(3, 6, dec_piece)
    stores = put_out(planes_x, raw_x, dec_hbm, out_sem)
    up.start_second()
    loop(0, 2, gi_piece)
    down.start_third()
    small.start_second()
    loop(2, 4, gi_piece)
    up.start_third()
    loop(4, 6, gi_piece)
    stores += put_out(planes_c, raw_c, gi_hbm, out_sem.at[pl.ds(4, 4)])
    down.finish(scale, down_out)
    stores.append(pltpu.make_async_copy(down_out, down_hbm, out_sem.at[8]))
    stores[-1].start()
    small.finish(scale, small_out)
    stores.append(pltpu.make_async_copy(small_out, small_hbm, out_sem.at[9]))
    stores[-1].start()
    up.finish(scale, up_out)
    stores.append(pltpu.make_async_copy(up_out, up_hbm, out_sem.at[10]))
    stores[-1].start()
    for copy in first + second + third:
        copy.wait_send()
    for each in (down, up, small):
        each.settle()
    for store in stores:
        store.wait()


def level(x, c, cov, wd, wu, kern, scale):
    hbm = pl.BlockSpec(memory_space=pl.ANY)
    wide = lambda rows: pltpu.VMEM((rows, WIDE, 128), F32)
    mat = lambda rows, cols=128: pltpu.VMEM((rows, cols), BF)
    dma = lambda n: pltpu.SemaphoreType.DMA((n,))
    tall = (ROWS + 1) * COLS
    planes = jax.ShapeDtypeStruct((64, 2, 2, ROWS, COLS), BF)
    scratch = (
        [mat(128, CELLS), mat(128, tall)] * 2
        + [mat(CELLS), mat(tall)] * 2
        + [mat(384, 256)] * 2
        + [pltpu.VMEM((ROWS, WIDE, 256), F32)] * 2
        + [wide(ROWS + 4), wide(ROWS + 2), wide(ROWS + 4), wide(ROWS + 2), wide(ROWS)]
        + [mat(tall, 256)] * 2
        + [pltpu.VMEM((4, REACH, 128), F32)]
        + [pltpu.VMEM((384, 128), F32)] * 2
        + [pltpu.VMEM((576, 128), F32)] * 2
        + [pltpu.VMEM((2, 1, 9), F32)]
        + [pltpu.VMEM((3, 16), jnp.int32), pltpu.VMEM((9, 64, 128), BF), pltpu.VMEM((9, 64, 128), BF)]
        + [pltpu.VMEM((9, 2, 128), F32)]
        + [pltpu.VMEM((4, 64, ROWS, COLS), BF)] * 2
        + [pltpu.VMEM((4, 64 * ROWS, COLS), F32)] * 2
        + [mat(384)] * 4
        + [mat(16)] * 2
        + [mat(128)] * 2
        + [pltpu.VMEM((200, 128), F32)] * 2
        + [mat(576)] * 4
        + [pltpu.VMEM((384, 256), F32), pltpu.VMEM((624, 128), F32), pltpu.VMEM((24, 128), F32)]
        + [dma(12), dma(11), dma(6), dma(6), dma(2), dma(2), dma(2), dma(2)]
        + sum_scratch()
        + sum_scratch()
        + small_scratch((24, 128))
    )
    return pl.pallas_call(
        functools.partial(kernel, scale),
        out_shape=(
            planes,
            planes,
            jax.ShapeDtypeStruct((576, 128), F32),
            jax.ShapeDtypeStruct((576, 128), F32),
            jax.ShapeDtypeStruct((2, 1, 9), F32),
        ),
        in_specs=[pl.BlockSpec(memory_space=pltpu.HBM)] * 6,
        out_specs=(hbm,) * 5,
        scratch_shapes=scratch,
        compiler_params=pltpu.CompilerParams(
            collective_id=0, has_side_effects=True, vmem_limit_bytes=56 * 1024 * 1024
        ),
        cost_estimate=pl.CostEstimate(flops=3_600_000_000, bytes_accessed=7_000_000, transcendentals=500_000),
    )(x, c, cov, wd, wu, kern)


def hand_on(dec, gi, down, up, small, *rest):
    outs, held, sems = rest[:5], rest[5:10], rest[10]
    moves = []
    for n, source in enumerate((dec, gi, down, up, small)):
        parts = 4 if n < 2 else 1
        size = source.shape[0] // parts
        for k in range(parts):
            at = pl.ds(k * size, size)
            spot = 4 * n + k
            moves.append(
                (
                    pltpu.make_async_copy(source.at[at], held[n].at[at], sems.at[0, spot]),
                    pltpu.make_async_copy(held[n].at[at], outs[n].at[at], sems.at[1, spot]),
                )
            )
    for load, store in moves:
        load.start()
    for load, store in moves:
        load.wait()
        store.start()
    for load, store in moves:
        store.wait()


def handed_on(*arrays):
    hbm = pl.BlockSpec(memory_space=pltpu.HBM)
    return pl.pallas_call(
        hand_on,
        out_shape=tuple(jax.ShapeDtypeStruct(a.shape, a.dtype) for a in arrays),
        in_specs=[hbm] * len(arrays),
        out_specs=(hbm,) * len(arrays),
        scratch_shapes=[pltpu.VMEM(a.shape, a.dtype) for a in arrays]
        + [pltpu.SemaphoreType.DMA((2, 4 * len(arrays)))],
        compiler_params=pltpu.CompilerParams(vmem_limit_bytes=60 * 1024 * 1024),
    )(*arrays)


def shards(inputs, kernels, w_down, w_up, cotangent, coverage):
    total = inputs.shape[3] * inputs.shape[4] * N_LAT * N_LON
    scale = 1.0 / math.sqrt(total)
    found = level(
        inputs,
        cotangent,
        coverage,
        jnp.transpose(w_down, (0, 2, 1)),
        w_up,
        jnp.transpose(kernels, (1, 0, 2)),
        scale,
    )
    decoded, grad_input, down, up, small = handed_on(*found)
    return (
        decoded,
        grad_input,
        jnp.transpose(down.reshape(9, 64, 128), (0, 2, 1)),
        up.reshape(9, 64, 128),
        jnp.transpose(small, (0, 2, 1)),
    )


def solution(mesh):
    placed = (
        P(None, None, None, "lat", "lon"),
        P(),
        P(),
        P(),
        P(None, None, None, "lat", "lon"),
        P("lat", "lon"),
    )
    return jax.shard_map(
        shards,
        mesh=mesh,
        in_specs=placed,
        out_specs=(
            P(None, None, None, "lat", "lon"),
            P(None, None, None, "lat", "lon"),
            P(),
            P(),
            P(None, None, ("lat", "lon")),
        ),
        check_vma=False,
    )
```

```python
import functools
import math

import jax
import jax.numpy as jnp
from jax import lax
from jax.experimental import pallas as pl
from jax.experimental.pallas import tpu as pltpu
from jax.sharding import PartitionSpec as P

BF = jnp.bfloat16
F32 = jnp.float32
ROWS = 24
COLS = 128
CELLS = ROWS * COLS
OFF = 16
WIDE = 160
LO = 8
SPAN = 144
REACH = 136
MESH = pl.DeviceIdType.MESH
N_LAT = 8
N_LON = 16
NEAR = 8
FAR = 16
PIECE = 72
PADDED = 80


def send(src, dst, send_sem, recv_sem, target):
    return pltpu.make_async_remote_copy(
        src_ref=src,
        dst_ref=dst,
        send_sem=send_sem,
        recv_sem=recv_sem,
        device_id=target,
        device_id_type=MESH,
    )


def greet(my_lat, my_lon):
    barrier = pltpu.get_barrier_semaphore()
    run, place, rank = my_lon // NEAR, lax.rem(my_lon, NEAR), my_lat * 2 + my_lon // NEAR
    peers = [(my_lat, run * NEAR + lax.rem(place + d, NEAR)) for d in range(1, NEAR)]
    for d in range(1, FAR):
        other = lax.rem(rank + d, FAR)
        peers.append((other // 2, lax.rem(other, 2) * NEAR + place))
    for side in (1, N_LON - 1):
        beside = lax.rem(my_lon + side, N_LON)
        peers += [(my_lat, beside), (lax.rem(my_lat + N_LAT - 1, N_LAT), beside)]
    for peer in peers:
        pl.semaphore_signal(barrier, inc=1, device_id=peer, device_id_type=MESH)
    return barrier, len(peers)


class Sum:
    def __init__(self, my_lat, my_lon, pieces, got, part, parts, whole, *sems):
        self.my_lat, self.run, self.place = my_lat, my_lon // NEAR, lax.rem(my_lon, NEAR)
        self.rank = my_lat * 2 + self.run
        self.pieces, self.got, self.part, self.parts, self.whole = pieces, got, part, parts, whole
        self.s1, self.r1, self.s2, self.r2, self.s3, self.r3 = sems

    def near(self, d):
        return (self.my_lat, self.run * NEAR + lax.rem(self.place + d, NEAR))

    def far(self, d):
        rank = lax.rem(self.rank + d, FAR)
        return (rank // 2, lax.rem(rank, 2) * NEAR + self.place)

    def first(self, d):
        peer = lax.rem(self.place + d, NEAR)
        return send(self.pieces.at[peer], self.got.at[d], self.s1, self.r1, self.near(d))

    def second(self, d):
        return send(self.part, self.parts.at[d], self.s2, self.r2, self.far(d))

    def third(self, d):
        return send(self.part, self.whole.at[d], self.s3, self.r3, self.near(d))

    def all_of(self, buffer, sent, received):
        arrived = buffer.at[pl.ds(1, buffer.shape[0] - 1)]
        return send(arrived, arrived, sent, received, self.near(1))

    def start_first(self):
        for d in range(1, NEAR):
            self.first(d).start()

    def start_second(self):
        self.all_of(self.got, self.s1, self.r1).wait_recv()
        total = self.pieces[self.place].astype(F32)
        for d in range(1, NEAR):
            total = total + self.got[d].astype(F32)
        rounded = total.astype(BF)
        self.part[...] = rounded
        self.parts[0] = rounded
        for d in range(1, FAR):
            self.second(d).start()

    def start_third(self):
        self.all_of(self.parts, self.s2, self.r2).wait()
        total = jnp.zeros((PADDED, 128), F32)
        for rank in range(FAR):
            total = total + self.parts[lax.rem(self.rank - rank + FAR, FAR)].astype(F32)
        rounded = total.astype(BF)
        self.part[...] = rounded
        self.whole[0] = rounded
        for d in range(1, NEAR):
            self.third(d).start()

    def extra(self, q):
        return self.whole[lax.rem(self.place - q + NEAR, NEAR)].astype(F32)[PIECE:]

    def finish(self, scale, out):
        self.all_of(self.whole, self.s3, self.r3).wait_recv()
        for d in range(NEAR):
            k = lax.rem(self.place - d + NEAR, NEAR)
            at = pl.ds(pl.multiple_of(k * PIECE, 8), PIECE)
            out[at, :] = self.whole[d].astype(F32)[:PIECE] * scale

    def settle(self):
        self.all_of(self.got, self.s1, self.r1).wait_send()
        self.all_of(self.whole, self.s3, self.r3).wait_send()


def sum_scratch():
    piece = lambda *lead: pltpu.VMEM(lead + (PADDED, 128), BF)
    buffers = [piece(NEAR), piece(NEAR), piece(), piece(FAR), piece(NEAR)]
    return buffers + [pltpu.SemaphoreType.DMA] * 6


def row_at(i):
    return pl.ds(pl.multiple_of(i * COLS, COLS), COLS)


def lay_weights(source, target):
    for a in range(3):
        top, mid, end = a * 128, a * 128 + 64, a * 128 + 128
        target[top:mid, 0:128] = source[3 * a + 1]
        target[mid:end, 0:128] = source[3 * a + 2]
        target[top:mid, 128:256] = jnp.zeros((64, 128), BF)
        target[mid:end, 128:256] = source[3 * a]


def own_channel(total, channel, scale, out):
    row = lax.broadcasted_iota(jnp.int32, total.shape, 0)
    lane = lax.broadcasted_iota(jnp.int32, total.shape, 1)
    column = jnp.sum(jnp.where(lane == channel, total, 0.0), axis=1, keepdims=True) * scale
    for t in range(2):
        line = jnp.sum(jnp.where(row == lane + 9 * t, column, 0.0), axis=0, keepdims=True)
        out[t] = line[:, 0:9]


def loop(low, high, body, wide=1):
    def step(n, carry):
        for k in range(wide):
            body(low + n * wide + k)
        return carry

    lax.fori_loop(0, (high - low) // wide, step, 0)


def plane_rows(i):
    return pl.ds(i, 64, stride=ROWS)


def taps_sum(field, row, base, coefs, first, rows_of, cols_of, span):
    acc = field[row, pl.ds(base, span), :]
    for a in range(3):
        for b in range(3):
            coef = coefs[3 * a + b, first : first + 1, :]
            acc = acc + coef * field[rows_of(a), pl.ds(cols_of(b), span), :]
    return acc


def kernel(
    scale, x_hbm, c_hbm, cov_hbm, wd_hbm, wu_hbm, kern_hbm,
    dec_hbm, gi_hbm, down_hbm, up_hbm, small_hbm,
    xa0, xa1, ma0, ma1, xb0, xb1, mb0, mb1, wdm, wum, yx, ym,
    s0, s1, r2, r1, ds_, d2, pg2, tmp, pack_l, pack_r,
    down_out, up_out, small_out, cov, wd, wu, kern, raw_x, raw_c, planes_x, planes_c, send_l, send_r, got_l, got_r, got_lc, got_rc, row_x, row_m,
    tile_l, tile_r, e2_up, e2_dn, got_up, got_dn, grad, flat, small_mine,
    in_sem, out_sem, e1_s, e1_r, e2_s, e2_r, e3_s, e3_r, *sums
):
    my_lat, my_lon = lax.axis_index("lat"), lax.axis_index("lon")
    up_lat, dn_lat = lax.rem(my_lat + N_LAT - 1, N_LAT), lax.rem(my_lat + 1, N_LAT)
    lt_lon, rt_lon = lax.rem(my_lon + N_LON - 1, N_LON), lax.rem(my_lon + 1, N_LON)
    has_up = (my_lat > 0).astype(F32)
    has_dn = (my_lat < N_LAT - 1).astype(F32)
    down = Sum(my_lat, my_lon, *sums[:11])
    up = Sum(my_lat, my_lon, *sums[11:22])

    loads = []
    for n, (source, raw) in enumerate(((x_hbm, raw_x), (c_hbm, raw_c))):
        for u in range(2):
            for v in range(2):
                p = 2 * u + v
                loads.append(
                    pltpu.make_async_copy(source.at[:, u, v], raw.at[p], in_sem.at[4 * n + p])
                )
    params = [
        pltpu.make_async_copy(source, target, in_sem.at[8 + n])
        for n, (source, target) in enumerate(
            ((cov_hbm, cov), (wd_hbm, wd), (wu_hbm, wu), (kern_hbm, kern))
        )
    ]
    for load in params + loads:
        load.start()
    barrier, met = greet(my_lat, my_lon)
    for load in params:
        load.wait()
    lay_weights(wd, wdm)
    lay_weights(wu, wum)
    spread = (
        lax.broadcasted_iota(jnp.int32, (16, COLS), 0)
        == lax.broadcasted_iota(jnp.int32, (16, COLS), 1) // 8
    ).astype(BF)
    flags = jnp.dot(cov[...].astype(F32).astype(BF), spread, preferred_element_type=F32).astype(BF)

    def unfold(raw, planes, p):
        def step(g):
            block = raw[p, pl.ds(g * 16, 16)].astype(F32)
            planes[p, pl.ds(pl.multiple_of(g * 384, 384), 384), :] = block.reshape(384, COLS)

        loop(0, 4, step)

    def turn(u, flag, planes, field, into, part, i):
        at = row_at(i + u)
        block = jnp.concatenate(
            [planes[2 * u, plane_rows(i), :], planes[2 * u + 1, plane_rows(i), :]], axis=0
        ).astype(BF)
        if flag is not None:
            block = block * flag
        field[:, at] = block
        block = block.T
        into[at, :] = block
        block = block.astype(F32)
        spot = u * 192 + i * 8 + part
        pack_l[pl.ds(spot, 4), :] = block[0:4]
        pack_r[pl.ds(spot, 4), :] = block[COLS - 4 : COLS]

    for u, field, into in ((0, xa0, xb0), (1, xa1, xb1)):
        for v in range(2):
            loads[2 * u + v].wait()
            unfold(raw_x, planes_x, 2 * u + v)
        loop(0, ROWS, functools.partial(turn, u, None, planes_x, field, into, 0), 4)
    for u, field, into in ((0, ma0, mb0), (1, ma1, mb1)):
        for v in range(2):
            loads[4 + 2 * u + v].wait()
            unfold(raw_c, planes_c, 2 * u + v)
        for q in range(3):
            body = functools.partial(turn, u, flags[q : q + 1, :], planes_c, field, into, 4)
            loop(8 * q, 8 * q + 8, body, 4)
    send_l[...] = pack_l[...].astype(BF)
    send_r[...] = pack_r[...].astype(BF)

    pl.semaphore_wait(barrier, met)
    last = pl.ds(ROWS * COLS, COLS)
    corner = pl.ds(368, 16)
    first = [
        send(send_l, got_r, e1_s.at[0], e1_r.at[0], (my_lat, lt_lon)),
        send(send_r, got_l, e1_s.at[1], e1_r.at[1], (my_lat, rt_lon)),
        send(send_l.at[corner], got_rc, e1_s.at[2], e1_r.at[2], (dn_lat, lt_lon)),
        send(send_r.at[corner], got_lc, e1_s.at[3], e1_r.at[3], (dn_lat, rt_lon)),
        send(xa1.at[:, last], row_x, e1_s.at[4], e1_r.at[4], (dn_lat, my_lon)),
        send(ma1.at[:, last], row_m, e1_s.at[5], e1_r.at[5], (dn_lat, my_lon)),
    ]
    for copy in first:
        copy.start()

    def conv_rows(i, count):
        here = pl.ds(pl.multiple_of(i * COLS, COLS), count * COLS)
        after = pl.ds(pl.multiple_of((i + 1) * COLS, COLS), count * COLS)
        for b0, b1, weight, y in ((xb0, xb1, wdm, yx), (mb0, mb1, wum, ym)):
            taps = jnp.concatenate([b1[here, :], b0[here, :], b1[after, :]], axis=1)
            found = jnp.dot(taps, weight[...], preferred_element_type=F32)
            for k in range(count):
                y[i + k, OFF : OFF + COLS, :] = found[k * COLS : (k + 1) * COLS]

    conv_rows(1, 3)
    loop(1, ROWS // 4, lambda n: conv_rows(4 * n, 4))

    def activate(i, low=LO, count=SPAN):
        span, before = pl.ds(low, count), pl.ds(low - 1, count)
        pre = yx[i, span, 0:128] + yx[i, before, 128:256]
        sig = 0.5 * jnp.tanh(0.5 * pre) + 0.5
        s0[i + 2, span, :] = (pre * sig).astype(BF).astype(F32)
        ds_[i, span, :] = sig * (1.0 + pre * (1.0 - sig))
        grad_row = ym[i, span, 0:128] + ym[i, before, 128:256]
        r2[i + 2, span, :] = grad_row.astype(BF).astype(F32)

    def rims(i):
        activate(i, LO, 16)
        activate(i, OFF + COLS, 8)

    loop(1, ROWS - 1, activate, 2)
    activate(ROWS - 1)

    for copy in first:
        copy.wait_recv()
    for got, field, into in ((row_x, xa1, xb1), (row_m, ma1, mb1)):
        row = got[...] * has_up.astype(BF)
        field[:, 0:COLS] = row
        into[0:COLS, :] = row.T
    conv_rows(0, 1)
    for got, edge, tile, at in ((got_l, got_lc, tile_l, 12), (got_r, got_rc, tile_r, 144)):
        tile[0:8, :] = edge[...].astype(F32)[8:16] * has_up
        tile[8:200, :] = got[192:384, :].astype(F32)
        taps = jnp.concatenate(
            [tile[0:192, :].astype(BF), got[0:192, :], tile[8:200, :].astype(BF)], axis=1
        )
        for weight, y, part in ((wdm, yx, 0), (wum, ym, 4)):
            rim = jnp.dot(taps, weight[...], preferred_element_type=F32)
            for i in range(ROWS):
                y[i, at : at + 4, :] = rim[i * 8 + part : i * 8 + part + 4]

    for i in (0, 1, ROWS - 2, ROWS - 1):
        rims(i) if i else activate(i)
    for n, field in enumerate((s0, r2)):
        for k in range(2):
            at = pl.ds(n * 288 + k * SPAN, SPAN)
            e2_up[at, :] = field[2 + k, LO : LO + SPAN, :].astype(BF)
            e2_dn[at, :] = field[ROWS + k, LO : LO + SPAN, :].astype(BF)
    second = [
        send(e2_up, got_up, e2_s.at[0], e2_r.at[0], (up_lat, my_lon)),
        send(e2_dn, got_dn, e2_s.at[1], e2_r.at[1], (dn_lat, my_lon)),
    ]
    for copy in second:
        copy.start()
    loop(2, ROWS - 2, rims, 4)

    def forward_1(r):
        acc = taps_sum(s0, r + 1, LO, kern, 0, lambda a: r + a, lambda b: LO - 1 + b, SPAN)
        s1[r, pl.ds(LO, SPAN), :] = acc

    def backward_1(r):
        acc = taps_sum(r2, r + 1, LO, kern, 1, lambda a: r - a + 2, lambda b: LO + 1 - b, SPAN)
        r1[r, pl.ds(LO, SPAN), :] = acc

    loop(2, ROWS, forward_1, 2)
    loop(2, ROWS, backward_1, 2)
    def pair(value, slot, into, i):
        slot = slot + lax.rem(i, 2)
        tmp[slot, 0:REACH, :] = value
        here = row_at(i)
        into[here, 0:128] = tmp[slot, 0:COLS, :].astype(BF)
        into[here, 128:256] = tmp[slot, 1 : COLS + 1, :].astype(BF)

    def backward_0(i):
        acc = taps_sum(r1, i + 1, OFF, kern, 0, lambda a: i - a + 2, lambda b: OFF + 1 - b, REACH)
        value = acc.astype(BF).astype(F32) * ds_[i, pl.ds(OFF, REACH), :]
        pair(value, 0, pg2, i)

    def forward_0(i):
        acc = taps_sum(s1, i + 1, OFF, kern, 1, lambda a: i + a, lambda b: OFF - 1 + b, REACH)
        pair(acc, 2, d2, i)

    loop(2, ROWS - 2, backward_0, 2)
    loop(2, ROWS - 2, forward_0, 2)
    for copy in second:
        copy.wait_recv()
    for n, field in enumerate((s0, r2)):
        for k in range(2):
            at = pl.ds(n * 288 + k * SPAN, SPAN)
            field[k, LO : LO + SPAN, :] = got_dn[at, :].astype(F32) * has_up
            field[ROWS + 2 + k, LO : LO + SPAN, :] = got_up[at, :].astype(F32) * has_dn
    for r in (0, 1, ROWS, ROWS + 1):
        forward_1(r)
        backward_1(r)
    for field in (s1, r1):
        field[0, LO : LO + SPAN, :] = field[0, LO : LO + SPAN, :] * has_up
        field[ROWS + 1, LO : LO + SPAN, :] = field[ROWS + 1, LO : LO + SPAN, :] * has_dn

    for i in (0, 1, ROWS - 2, ROWS - 1):
        backward_0(i)
        forward_0(i)
    third = [
        send(pg2.at[pl.ds(0, COLS)], pg2.at[pl.ds(CELLS, COLS)], e3_s.at[0], e3_r.at[0], (up_lat, my_lon)),
        send(d2.at[pl.ds(0, COLS)], d2.at[pl.ds(CELLS, COLS)], e3_s.at[1], e3_r.at[1], (up_lat, my_lon)),
    ]
    for copy in third:
        copy.start()

    def weight_grad(a0, a1, pairs, total):
        half = CELLS // 2
        for n in range(2):
            at, after = pl.ds(n * half, half), pl.ds(n * half + COLS, half)
            taps = jnp.concatenate([a1[:, at], a0[:, at], a1[:, after]], axis=0)
            part = jnp.dot(taps, pairs[at, :], preferred_element_type=F32)
            grad[...] = part if n == 0 else grad[...] + part
        for a in range(3):
            top, mid, end = a * 128, a * 128 + 64, a * 128 + 128
            flat[(3 * a + 1) * 64 : (3 * a + 2) * 64, :] = grad[top:mid, 0:128]
            flat[(3 * a + 2) * 64 : (3 * a + 3) * 64, :] = grad[mid:end, 0:128]
            flat[3 * a * 64 : (3 * a + 1) * 64, :] = grad[mid:end, 128:256]
        for k in range(NEAR):
            total.pieces[k] = flat[pl.ds(k * PIECE, PADDED), :].astype(BF)

    def kernel_grad(left, left_row, right, right_row, first_row):
        def step(i, accs):
            own = left[i + left_row, OFF : OFF + COLS, :]
            found = []
            for a in range(3):
                for b in range(3):
                    other = right[i + a + right_row, pl.ds(OFF - 1 + b, COLS), :]
                    found.append(accs[3 * a + b] + jnp.sum((own * other).reshape(16, 8, 128), axis=0))
            return tuple(found)

        accs = lax.fori_loop(0, ROWS, step, tuple(jnp.zeros((8, 128), F32) for _ in range(9)))
        for t in range(9):
            small_mine[first_row + t : first_row + t + 1, :] = jnp.sum(accs[t], axis=0, keepdims=True)

    flat[576:584, :] = jnp.zeros((8, 128), F32)
    weight_grad(xa0, xa1, pg2, down)
    down.start_first()
    small_mine[16:24, :] = jnp.zeros((8, 128), F32)
    kernel_grad(r1, 1, s0, 1, 0)
    kernel_grad(r2, 2, s1, 0, 9)
    weight_grad(ma0, ma1, d2, up)
    for q in range(3):
        rows = flat[q * PIECE : (q + 1) * PIECE, :], small_mine[q * 8 : (q + 1) * 8, :]
        up.pieces[q] = jnp.concatenate(rows, axis=0).astype(BF)
    up.start_first()

    def add_piece(weight, pairs, f0, f1, planes, n):
        at = pl.ds(pl.multiple_of(n * 512, 512), 512)
        after = pl.ds(pl.multiple_of(n * 512 + COLS, COLS), 512)
        lines = jnp.concatenate([pairs[row_at(4 * n + k), :].T for k in range(5)], axis=1)
        found = jnp.dot(weight[128:384, :], lines[:, 0:512], preferred_element_type=F32)
        under = jnp.dot(weight[0:128, :], lines[:, COLS:640], preferred_element_type=F32)
        even = f0[:, at].astype(F32) + found[0:128]
        odd = f1[:, after].astype(F32) + found[128:256] + under
        for u, value in ((0, even), (1, odd)):
            for k in range(4):
                for v in range(2):
                    planes[2 * u + v, plane_rows(4 * n + k), :] = value[
                        v * 64 : (v + 1) * 64, k * COLS : (k + 1) * COLS
                    ]

    def put_out(planes, raw, out, sem):
        stores = []
        for u in range(2):
            for v in range(2):
                p = 2 * u + v

                def fold(g, p=p):
                    block = planes[p, pl.ds(pl.multiple_of(g * 384, 384), 384), :]
                    raw[p, pl.ds(g * 16, 16)] = block.astype(BF).reshape(16, ROWS, COLS)

                loop(0, 4, fold)
                stores.append(pltpu.make_async_copy(raw.at[p], out.at[:, u, v], sem.at[p]))
                stores[-1].start()
        return stores

    dec_piece = functools.partial(add_piece, wum, d2, xa0, xa1, planes_x)
    gi_piece = functools.partial(add_piece, wdm, pg2, ma0, ma1, planes_c)
    below = pl.ds(CELLS, COLS)

    down.start_second()
    loop(0, 3, dec_piece)
    up.start_second()
    for copy, field in zip(third, (pg2, d2)):
        copy.wait_recv()
        field[below, :] = field[below, :] * has_dn.astype(BF)
    loop(3, 6, dec_piece)
    stores = put_out(planes_x, raw_x, dec_hbm, out_sem)
    down.start_third()
    loop(0, 4, gi_piece)
    up.start_third()
    loop(4, 6, gi_piece)
    stores += put_out(planes_c, raw_c, gi_hbm, out_sem.at[pl.ds(4, 4)])
    down.finish(scale, down_out)
    stores.append(pltpu.make_async_copy(down_out, down_hbm, out_sem.at[8]))
    stores[-1].start()
    up.finish(scale, up_out)
    stores.append(pltpu.make_async_copy(up_out, up_hbm, out_sem.at[10]))
    stores[-1].start()
    for q in range(3):
        small_mine[q * 8 : (q + 1) * 8, :] = up.extra(q)
    own_channel(small_mine[...], my_lat * N_LON + my_lon, scale, small_out)
    stores.append(pltpu.make_async_copy(small_out, small_hbm, out_sem.at[9]))
    stores[-1].start()
    for copy in first + second + third:
        copy.wait_send()
    for each in (down, up):
        each.settle()
    for store in stores:
        store.wait()


def level(x, c, cov, wd, wu, kern, scale):
    hbm = pl.BlockSpec(memory_space=pl.ANY)
    wide = lambda rows: pltpu.VMEM((rows, WIDE, 128), F32)
    mat = lambda rows, cols=128: pltpu.VMEM((rows, cols), BF)
    dma = lambda n: pltpu.SemaphoreType.DMA((n,))
    tall = (ROWS + 1) * COLS
    planes = jax.ShapeDtypeStruct((64, 2, 2, ROWS, COLS), BF)
    scratch = (
        [mat(128, CELLS), mat(128, tall)] * 2
        + [mat(CELLS), mat(tall)] * 2
        + [mat(384, 256)] * 2
        + [pltpu.VMEM((ROWS, WIDE, 256), F32)] * 2
        + [wide(ROWS + 4), wide(ROWS + 2), wide(ROWS + 4), wide(ROWS + 2), wide(ROWS)]
        + [mat(tall, 256)] * 2
        + [pltpu.VMEM((4, REACH, 128), F32)]
        + [pltpu.VMEM((384, 128), F32)] * 2
        + [pltpu.VMEM((576, 128), F32)] * 2
        + [pltpu.VMEM((2, 1, 9), F32)]
        + [pltpu.VMEM((3, 16), jnp.int32), pltpu.VMEM((9, 64, 128), BF), pltpu.VMEM((9, 64, 128), BF)]
        + [pltpu.VMEM((9, 2, 128), F32)]
        + [pltpu.VMEM((4, 64, ROWS, COLS), BF)] * 2
        + [pltpu.VMEM((4, 64 * ROWS, COLS), F32)] * 2
        + [mat(384)] * 4
        + [mat(16)] * 2
        + [mat(128)] * 2
        + [pltpu.VMEM((200, 128), F32)] * 2
        + [mat(576)] * 4
        + [pltpu.VMEM((384, 256), F32), pltpu.VMEM((584, 128), F32), pltpu.VMEM((24, 128), F32)]
        + [dma(12), dma(11), dma(6), dma(6), dma(2), dma(2), dma(2), dma(2)]
        + sum_scratch()
        + sum_scratch()
    )
    return pl.pallas_call(
        functools.partial(kernel, scale),
        out_shape=(
            planes,
            planes,
            jax.ShapeDtypeStruct((576, 128), F32),
            jax.ShapeDtypeStruct((576, 128), F32),
            jax.ShapeDtypeStruct((2, 1, 9), F32),
        ),
        in_specs=[pl.BlockSpec(memory_space=pltpu.HBM)] * 6,
        out_specs=(hbm,) * 5,
        scratch_shapes=scratch,
        compiler_params=pltpu.CompilerParams(
            collective_id=0, has_side_effects=True, vmem_limit_bytes=46 * 1024 * 1024
        ),
        cost_estimate=pl.CostEstimate(flops=3_600_000_000, bytes_accessed=7_000_000, transcendentals=500_000),
    )(*(pltpu.with_memory_space_constraint(v, pltpu.HBM) for v in (x, c, cov, wd, wu, kern)))


def hand_on(*refs):
    count = len(refs) // 2
    sems = refs[-1]
    copies = [
        pltpu.make_async_copy(source, target, sems.at[n])
        for n, (source, target) in enumerate(zip(refs[:count], refs[count : 2 * count]))
    ]
    for copy in copies:
        copy.start()
    for copy in copies:
        copy.wait()


def handed_on(*arrays):
    vmem = pl.BlockSpec(memory_space=pltpu.VMEM)
    hbm = pl.BlockSpec(memory_space=pltpu.HBM)
    return pl.pallas_call(
        hand_on,
        out_shape=tuple(jax.ShapeDtypeStruct(a.shape, a.dtype) for a in arrays),
        in_specs=[vmem] * len(arrays),
        out_specs=(hbm,) * len(arrays),
        scratch_shapes=[pltpu.SemaphoreType.DMA((len(arrays),))],
        compiler_params=pltpu.CompilerParams(vmem_limit_bytes=16 * 1024 * 1024),
    )(*arrays)


def shards(inputs, kernels, w_down, w_up, cotangent, coverage):
    total = inputs.shape[3] * inputs.shape[4] * N_LAT * N_LON
    scale = 1.0 / math.sqrt(total)
    found = level(
        inputs,
        cotangent,
        coverage,
        jnp.transpose(w_down, (0, 2, 1)),
        w_up,
        jnp.transpose(kernels, (1, 0, 2)),
        scale,
    )
    decoded, grad_input, down, up, small = handed_on(*found)
    return (
        decoded,
        grad_input,
        jnp.transpose(down.reshape(9, 64, 128), (0, 2, 1)),
        up.reshape(9, 64, 128),
        jnp.transpose(small, (0, 2, 1)),
    )


def solution(mesh):
    placed = (
        P(None, None, None, "lat", "lon"),
        P(),
        P(),
        P(),
        P(None, None, None, "lat", "lon"),
        P("lat", "lon"),
    )
    return jax.shard_map(
        shards,
        mesh=mesh,
        in_specs=placed,
        out_specs=(
            P(None, None, None, "lat", "lon"),
            P(None, None, None, "lat", "lon"),
            P(),
            P(),
            P(None, None, ("lat", "lon")),
        ),
        check_vma=False,
    )
```

```python
import functools
import math

import jax
import jax.numpy as jnp
from jax import lax
from jax.experimental import pallas as pl
from jax.experimental.pallas import tpu as pltpu
from jax.sharding import PartitionSpec as P

BF = jnp.bfloat16
F32 = jnp.float32
ROWS = 24
COLS = 128
CELLS = ROWS * COLS
OFF = 16
WIDE = 160
LO = 8
SPAN = 144
REACH = 136
MESH = pl.DeviceIdType.MESH
N_LAT = 8
N_LON = 16
NEAR = 8
FAR = 16
PIECE = 72
PADDED = 80


def send(src, dst, send_sem, recv_sem, target):
    return pltpu.make_async_remote_copy(
        src_ref=src,
        dst_ref=dst,
        send_sem=send_sem,
        recv_sem=recv_sem,
        device_id=target,
        device_id_type=MESH,
    )


def greet(my_lat, my_lon):
    barrier = pltpu.get_barrier_semaphore()
    run, place, rank = my_lon // NEAR, lax.rem(my_lon, NEAR), my_lat * 2 + my_lon // NEAR
    peers = [(my_lat, run * NEAR + lax.rem(place + d, NEAR)) for d in range(1, NEAR)]
    for d in range(1, FAR):
        other = lax.rem(rank + d, FAR)
        peers.append((other // 2, lax.rem(other, 2) * NEAR + place))
    for side in (1, N_LON - 1):
        beside = lax.rem(my_lon + side, N_LON)
        peers += [(my_lat, beside), (lax.rem(my_lat + N_LAT - 1, N_LAT), beside)]
    for peer in peers:
        pl.semaphore_signal(barrier, inc=1, device_id=peer, device_id_type=MESH)
    return barrier, len(peers)


class Sum:
    def __init__(self, my_lat, my_lon, pieces, got, part, parts, whole, *sems):
        self.my_lat, self.run, self.place = my_lat, my_lon // NEAR, lax.rem(my_lon, NEAR)
        self.rank = my_lat * 2 + self.run
        self.pieces, self.got, self.part, self.parts, self.whole = pieces, got, part, parts, whole
        self.s1, self.r1, self.s2, self.r2, self.s3, self.r3 = sems

    def near(self, d):
        return (self.my_lat, self.run * NEAR + lax.rem(self.place + d, NEAR))

    def far(self, d):
        rank = lax.rem(self.rank + d, FAR)
        return (rank // 2, lax.rem(rank, 2) * NEAR + self.place)

    def first(self, d):
        peer = lax.rem(self.place + d, NEAR)
        return send(self.pieces.at[peer], self.got.at[d], self.s1, self.r1, self.near(d))

    def second(self, d):
        return send(self.part, self.parts.at[d], self.s2, self.r2, self.far(d))

    def third(self, d):
        return send(self.part, self.whole.at[d], self.s3, self.r3, self.near(d))

    def all_of(self, buffer, sent, received):
        arrived = buffer.at[pl.ds(1, buffer.shape[0] - 1)]
        return send(arrived, arrived, sent, received, self.near(1))

    def start_first(self):
        for d in range(1, NEAR):
            self.first(d).start()

    def start_second(self):
        self.all_of(self.got, self.s1, self.r1).wait_recv()
        total = self.pieces[self.place].astype(F32)
        for d in range(1, NEAR):
            total = total + self.got[d].astype(F32)
        rounded = total.astype(BF)
        self.part[...] = rounded
        self.parts[0] = rounded
        for d in range(1, FAR):
            self.second(d).start()

    def start_third(self):
        self.all_of(self.parts, self.s2, self.r2).wait()
        total = jnp.zeros((PADDED, 128), F32)
        for rank in range(FAR):
            total = total + self.parts[lax.rem(self.rank - rank + FAR, FAR)].astype(F32)
        rounded = total.astype(BF)
        self.part[...] = rounded
        self.whole[0] = rounded
        for d in range(1, NEAR):
            self.third(d).start()

    def extra(self, q):
        return self.whole[lax.rem(self.place - q + NEAR, NEAR)].astype(F32)[PIECE:]

    def finish(self, scale, out):
        self.all_of(self.whole, self.s3, self.r3).wait_recv()
        for d in range(NEAR):
            k = lax.rem(self.place - d + NEAR, NEAR)
            at = pl.ds(pl.multiple_of(k * PIECE, 8), PIECE)
            out[at, :] = self.whole[d].astype(F32)[:PIECE] * scale

    def settle(self):
        self.all_of(self.got, self.s1, self.r1).wait_send()
        self.all_of(self.whole, self.s3, self.r3).wait_send()


def sum_scratch():
    piece = lambda *lead: pltpu.VMEM(lead + (PADDED, 128), BF)
    buffers = [piece(NEAR), piece(NEAR), piece(), piece(FAR), piece(NEAR)]
    return buffers + [pltpu.SemaphoreType.DMA] * 6


def row_at(i):
    return pl.ds(pl.multiple_of(i * COLS, COLS), COLS)


def lay_weights(source, target):
    for a in range(3):
        top, mid, end = a * 128, a * 128 + 64, a * 128 + 128
        target[top:mid, 0:128] = source[3 * a + 1]
        target[mid:end, 0:128] = source[3 * a + 2]
        target[top:mid, 128:256] = jnp.zeros((64, 128), BF)
        target[mid:end, 128:256] = source[3 * a]


def own_channel(total, channel, scale, out):
    row = lax.broadcasted_iota(jnp.int32, total.shape, 0)
    lane = lax.broadcasted_iota(jnp.int32, total.shape, 1)
    column = jnp.sum(jnp.where(lane == channel, total, 0.0), axis=1, keepdims=True) * scale
    for t in range(2):
        line = jnp.sum(jnp.where(row == lane + 9 * t, column, 0.0), axis=0, keepdims=True)
        out[t] = line[:, 0:9]


def loop(low, high, body, wide=1):
    def step(n, carry):
        for k in range(wide):
            body(low + n * wide + k)
        return carry

    lax.fori_loop(0, (high - low) // wide, step, 0)


def plane_rows(i):
    return pl.ds(i, 64, stride=ROWS)


def taps_sum(field, coefs, first, rows_of, cols_of, span):
    total = None
    for a in range(3):
        for b in range(3):
            coef = coefs[3 * a + b, first : first + 1, :]
            term = coef * field[rows_of(a), pl.ds(cols_of(b), span), :]
            total = term if total is None else total + term
    return total


def kernel(
    scale, x_hbm, c_hbm, cov_hbm, wd_hbm, wu_hbm, kern_hbm,
    dec_hbm, gi_hbm, down_hbm, up_hbm, small_hbm,
    xa0, xa1, ma0, ma1, xb0, xb1, mb0, mb1, wdm, wum, yx, ym,
    s0, s1, r2, r1, ds_, d2, pg2, tmp, pack_l, pack_r,
    down_out, up_out, small_out, cov, wd, wu, kern, raw_x, raw_c, planes_x, planes_c, send_l, send_r, got_l, got_r, got_lc, got_rc, row_x, row_m,
    tile_l, tile_r, e2_up, e2_dn, got_up, got_dn, grad, flat, small_mine,
    in_sem, out_sem, e1_s, e1_r, e2_s, e2_r, e3_s, e3_r, *sums
):
    my_lat, my_lon = lax.axis_index("lat"), lax.axis_index("lon")
    up_lat, dn_lat = lax.rem(my_lat + N_LAT - 1, N_LAT), lax.rem(my_lat + 1, N_LAT)
    lt_lon, rt_lon = lax.rem(my_lon + N_LON - 1, N_LON), lax.rem(my_lon + 1, N_LON)
    has_up = (my_lat > 0).astype(F32)
    has_dn = (my_lat < N_LAT - 1).astype(F32)
    down = Sum(my_lat, my_lon, *sums[:11])
    up = Sum(my_lat, my_lon, *sums[11:22])

    loads = []
    for n, (source, raw) in enumerate(((x_hbm, raw_x), (c_hbm, raw_c))):
        for u in range(2):
            for v in range(2):
                p = 2 * u + v
                loads.append(
                    pltpu.make_async_copy(source.at[:, u, v], raw.at[p], in_sem.at[4 * n + p])
                )
    params = [
        pltpu.make_async_copy(source, target, in_sem.at[8 + n])
        for n, (source, target) in enumerate(
            ((cov_hbm, cov), (wd_hbm, wd), (wu_hbm, wu), (kern_hbm, kern))
        )
    ]
    for load in params + loads:
        load.start()
    barrier, met = greet(my_lat, my_lon)
    for load in params:
        load.wait()
    kern[4] = kern[4] + 1.0
    lay_weights(wd, wdm)
    lay_weights(wu, wum)
    spread = (
        lax.broadcasted_iota(jnp.int32, (16, COLS), 0)
        == lax.broadcasted_iota(jnp.int32, (16, COLS), 1) // 8
    ).astype(BF)
    flags = jnp.dot(cov[...].astype(F32).astype(BF), spread, preferred_element_type=F32).astype(BF)

    def unfold(raw, planes, p):
        def step(g):
            block = raw[p, pl.ds(g * 16, 16)].astype(F32)
            planes[p, pl.ds(pl.multiple_of(g * 384, 384), 384), :] = block.reshape(384, COLS)

        loop(0, 4, step)

    def turn(u, flag, planes, field, into, part, i):
        at = row_at(i + u)
        block = jnp.concatenate(
            [planes[2 * u, plane_rows(i), :], planes[2 * u + 1, plane_rows(i), :]], axis=0
        ).astype(BF)
        if flag is not None:
            block = block * flag
        field[:, at] = block
        block = block.T
        into[at, :] = block
        block = block.astype(F32)
        spot = u * 192 + i * 8 + part
        pack_l[pl.ds(spot, 4), :] = block[0:4]
        pack_r[pl.ds(spot, 4), :] = block[COLS - 4 : COLS]

    for u, field, into in ((0, xa0, xb0), (1, xa1, xb1)):
        for v in range(2):
            loads[2 * u + v].wait()
            unfold(raw_x, planes_x, 2 * u + v)
        loop(0, ROWS, functools.partial(turn, u, None, planes_x, field, into, 0), 4)
    for u, field, into in ((0, ma0, mb0), (1, ma1, mb1)):
        for v in range(2):
            loads[4 + 2 * u + v].wait()
            unfold(raw_c, planes_c, 2 * u + v)
        for q in range(3):
            body = functools.partial(turn, u, flags[q : q + 1, :], planes_c, field, into, 4)
            loop(8 * q, 8 * q + 8, body, 4)
    send_l[...] = pack_l[...].astype(BF)
    send_r[...] = pack_r[...].astype(BF)

    pl.semaphore_wait(barrier, met)
    last = pl.ds(ROWS * COLS, COLS)
    corner = pl.ds(368, 16)
    first = [
        send(send_l, got_r, e1_s.at[0], e1_r.at[0], (my_lat, lt_lon)),
        send(send_r, got_l, e1_s.at[1], e1_r.at[1], (my_lat, rt_lon)),
        send(send_l.at[corner], got_rc, e1_s.at[2], e1_r.at[2], (dn_lat, lt_lon)),
        send(send_r.at[corner], got_lc, e1_s.at[3], e1_r.at[3], (dn_lat, rt_lon)),
        send(xa1.at[:, last], row_x, e1_s.at[4], e1_r.at[4], (dn_lat, my_lon)),
        send(ma1.at[:, last], row_m, e1_s.at[5], e1_r.at[5], (dn_lat, my_lon)),
    ]
    for copy in first:
        copy.start()

    def conv_rows(i, count):
        here = pl.ds(pl.multiple_of(i * COLS, COLS), count * COLS)
        after = pl.ds(pl.multiple_of((i + 1) * COLS, COLS), count * COLS)
        for b0, b1, weight, y in ((xb0, xb1, wdm, yx), (mb0, mb1, wum, ym)):
            taps = jnp.concatenate([b1[here, :], b0[here, :], b1[after, :]], axis=1)
            found = jnp.dot(taps, weight[...], preferred_element_type=F32)
            for k in range(count):
                y[i + k, OFF : OFF + COLS, :] = found[k * COLS : (k + 1) * COLS]

    conv_rows(1, 3)
    loop(1, ROWS // 4, lambda n: conv_rows(4 * n, 4))

    def activate(i, low=LO, count=SPAN):
        span, before = pl.ds(low, count), pl.ds(low - 1, count)
        pre = yx[i, span, 0:128] + yx[i, before, 128:256]
        sig = 0.5 * jnp.tanh(0.5 * pre) + 0.5
        s0[i + 2, span, :] = (pre * sig).astype(BF).astype(F32)
        ds_[i, span, :] = sig * (1.0 + pre * (1.0 - sig))
        grad_row = ym[i, span, 0:128] + ym[i, before, 128:256]
        r2[i + 2, span, :] = grad_row.astype(BF).astype(F32)

    def rims(i):
        activate(i, LO, 16)
        activate(i, OFF + COLS, 8)

    loop(1, ROWS - 1, activate, 2)
    activate(ROWS - 1)

    for copy in first:
        copy.wait_recv()
    for got, field, into in ((row_x, xa1, xb1), (row_m, ma1, mb1)):
        row = got[...] * has_up.astype(BF)
        field[:, 0:COLS] = row
        into[0:COLS, :] = row.T
    conv_rows(0, 1)
    for got, edge, tile, at in ((got_l, got_lc, tile_l, 12), (got_r, got_rc, tile_r, 144)):
        tile[0:8, :] = edge[...].astype(F32)[8:16] * has_up
        tile[8:200, :] = got[192:384, :].astype(F32)
        taps = jnp.concatenate(
            [tile[0:192, :].astype(BF), got[0:192, :], tile[8:200, :].astype(BF)], axis=1
        )
        for weight, y, part in ((wdm, yx, 0), (wum, ym, 4)):
            rim = jnp.dot(taps, weight[...], preferred_element_type=F32)
            for i in range(ROWS):
                y[i, at : at + 4, :] = rim[i * 8 + part : i * 8 + part + 4]

    for i in (0, 1, ROWS - 2, ROWS - 1):
        rims(i) if i else activate(i)
    for n, field in enumerate((s0, r2)):
        for k in range(2):
            at = pl.ds(n * 288 + k * SPAN, SPAN)
            e2_up[at, :] = field[2 + k, LO : LO + SPAN, :].astype(BF)
            e2_dn[at, :] = field[ROWS + k, LO : LO + SPAN, :].astype(BF)
    second = [
        send(e2_up, got_up, e2_s.at[0], e2_r.at[0], (up_lat, my_lon)),
        send(e2_dn, got_dn, e2_s.at[1], e2_r.at[1], (dn_lat, my_lon)),
    ]
    for copy in second:
        copy.start()
    loop(2, ROWS - 2, rims, 4)

    def forward_1(r):
        acc = taps_sum(s0, kern, 0, lambda a: r + a, lambda b: LO - 1 + b, SPAN)
        s1[r, pl.ds(LO, SPAN), :] = acc

    def backward_1(r):
        acc = taps_sum(r2, kern, 1, lambda a: r - a + 2, lambda b: LO + 1 - b, SPAN)
        r1[r, pl.ds(LO, SPAN), :] = acc

    loop(2, ROWS, forward_1, 2)
    loop(2, ROWS, backward_1, 2)
    def pair(value, slot, into, i):
        slot = slot + lax.rem(i, 2)
        tmp[slot, 0:REACH, :] = value
        here = row_at(i)
        into[here, 0:128] = tmp[slot, 0:COLS, :].astype(BF)
        into[here, 128:256] = tmp[slot, 1 : COLS + 1, :].astype(BF)

    def backward_0(i):
        acc = taps_sum(r1, kern, 0, lambda a: i - a + 2, lambda b: OFF + 1 - b, REACH)
        value = acc.astype(BF).astype(F32) * ds_[i, pl.ds(OFF, REACH), :]
        pair(value, 0, pg2, i)

    def forward_0(i):
        acc = taps_sum(s1, kern, 1, lambda a: i + a, lambda b: OFF - 1 + b, REACH)
        pair(acc, 2, d2, i)

    loop(2, ROWS - 2, backward_0, 2)
    grad[...] = jnp.zeros_like(grad)

    def add_grad(a0, a1, pairs, row, count):
        at = pl.ds(pl.multiple_of(row * COLS, COLS), count * COLS)
        after = pl.ds(pl.multiple_of((row + 1) * COLS, COLS), count * COLS)
        taps = jnp.concatenate([a1[:, at], a0[:, at], a1[:, after]], axis=0)
        grad[...] += jnp.dot(taps, pairs[at, :], preferred_element_type=F32)

    def forward_and_grad(n):
        add_grad(xa0, xa1, pg2, 4 + 4 * n, 4)
        for k in range(5):
            forward_0(2 + 5 * n + k)

    loop(0, 4, forward_and_grad)
    for copy in second:
        copy.wait_recv()
    for n, field in enumerate((s0, r2)):
        for k in range(2):
            at = pl.ds(n * 288 + k * SPAN, SPAN)
            field[k, LO : LO + SPAN, :] = got_dn[at, :].astype(F32) * has_up
            field[ROWS + 2 + k, LO : LO + SPAN, :] = got_up[at, :].astype(F32) * has_dn
    for r in (0, 1, ROWS, ROWS + 1):
        forward_1(r)
        backward_1(r)
    for field in (s1, r1):
        field[0, LO : LO + SPAN, :] = field[0, LO : LO + SPAN, :] * has_up
        field[ROWS + 1, LO : LO + SPAN, :] = field[ROWS + 1, LO : LO + SPAN, :] * has_dn

    for i in (0, 1, ROWS - 2, ROWS - 1):
        backward_0(i)
        forward_0(i)
    third = [
        send(pg2.at[pl.ds(0, COLS)], pg2.at[pl.ds(CELLS, COLS)], e3_s.at[0], e3_r.at[0], (up_lat, my_lon)),
        send(d2.at[pl.ds(0, COLS)], d2.at[pl.ds(CELLS, COLS)], e3_s.at[1], e3_r.at[1], (up_lat, my_lon)),
    ]

    def lay_pieces(total):
        for a in range(3):
            top, mid, end = a * 128, a * 128 + 64, a * 128 + 128
            flat[(3 * a + 1) * 64 : (3 * a + 2) * 64, :] = grad[top:mid, 0:128]
            flat[(3 * a + 2) * 64 : (3 * a + 3) * 64, :] = grad[mid:end, 0:128]
            flat[3 * a * 64 : (3 * a + 1) * 64, :] = grad[mid:end, 128:256]
        for k in range(NEAR):
            total.pieces[k] = flat[pl.ds(k * PIECE, PADDED), :].astype(BF)

    flat[576:584, :] = jnp.zeros((8, 128), F32)
    small_mine[16:24, :] = jnp.zeros((8, 128), F32)
    add_grad(xa0, xa1, pg2, 0, 4)
    add_grad(xa0, xa1, pg2, ROWS - 4, 4)
    lay_pieces(down)
    down.start_first()
    for copy in third:
        copy.start()

    def kernel_terms(own, other, accs):
        found = []
        for a in range(3):
            for b in range(3):
                near_by = other(a)[pl.ds(OFF - 1 + b, COLS), :]
                found.append(accs[3 * a + b] + jnp.sum((own * near_by).reshape(16, 8, 128), axis=0))
        return found

    def up_step(n, accs):
        add_grad(ma0, ma1, d2, 8 * n, 8)
        accs = list(accs)
        for k in range(8):
            i = 8 * n + k
            own = r1[i + 1, OFF : OFF + COLS, :]
            accs[:9] = kernel_terms(own, lambda a: s0.at[i + a + 1], accs[:9])
            own = r2[i + 2, OFF : OFF + COLS, :]
            accs[9:] = kernel_terms(own, lambda a: s1.at[i + a], accs[9:])
        return tuple(accs)

    grad[...] = jnp.zeros_like(grad)
    accs = lax.fori_loop(0, 3, up_step, tuple(jnp.zeros((8, 128), F32) for _ in range(18)))
    for t in range(18):
        small_mine[t : t + 1, :] = jnp.sum(accs[t], axis=0, keepdims=True)
    lay_pieces(up)
    for q in range(3):
        rows = flat[q * PIECE : (q + 1) * PIECE, :], small_mine[q * 8 : (q + 1) * 8, :]
        up.pieces[q] = jnp.concatenate(rows, axis=0).astype(BF)
    up.start_first()

    def add_piece(weight, pairs, f0, f1, planes, n):
        at = pl.ds(pl.multiple_of(n * 512, 512), 512)
        after = pl.ds(pl.multiple_of(n * 512 + COLS, COLS), 512)
        lines = jnp.concatenate([pairs[row_at(4 * n + k), :].T for k in range(5)], axis=1)
        found = jnp.dot(weight[128:384, :], lines[:, 0:512], preferred_element_type=F32)
        under = jnp.dot(weight[0:128, :], lines[:, COLS:640], preferred_element_type=F32)
        even = f0[:, at].astype(F32) + found[0:128]
        odd = f1[:, after].astype(F32) + found[128:256] + under
        for u, value in ((0, even), (1, odd)):
            for k in range(4):
                for v in range(2):
                    planes[2 * u + v, plane_rows(4 * n + k), :] = value[
                        v * 64 : (v + 1) * 64, k * COLS : (k + 1) * COLS
                    ]

    def put_out(planes, raw, out, sem):
        stores = []
        for u in range(2):
            for v in range(2):
                p = 2 * u + v

                def fold(g, p=p):
                    block = planes[p, pl.ds(pl.multiple_of(g * 384, 384), 384), :]
                    raw[p, pl.ds(g * 16, 16)] = block.astype(BF).reshape(16, ROWS, COLS)

                loop(0, 4, fold)
                stores.append(pltpu.make_async_copy(raw.at[p], out.at[:, u, v], sem.at[p]))
                stores[-1].start()
        return stores

    dec_piece = functools.partial(add_piece, wum, d2, xa0, xa1, planes_x)
    gi_piece = functools.partial(add_piece, wdm, pg2, ma0, ma1, planes_c)
    below = pl.ds(CELLS, COLS)

    loop(0, 1, dec_piece)
    down.start_second()
    for copy, field in zip(third, (pg2, d2)):
        copy.wait_recv()
        field[below, :] = field[below, :] * has_dn.astype(BF)
    loop(1, 6, dec_piece)
    stores = put_out(planes_x, raw_x, dec_hbm, out_sem)
    up.start_second()
    loop(0, 6, gi_piece)
    stores += put_out(planes_c, raw_c, gi_hbm, out_sem.at[pl.ds(4, 4)])
    down.start_third()
    up.start_third()
    down.finish(scale, down_out)
    stores.append(pltpu.make_async_copy(down_out, down_hbm, out_sem.at[8]))
    stores[-1].start()
    up.finish(scale, up_out)
    stores.append(pltpu.make_async_copy(up_out, up_hbm, out_sem.at[10]))
    stores[-1].start()
    for q in range(3):
        small_mine[q * 8 : (q + 1) * 8, :] = up.extra(q)
    own_channel(small_mine[...], my_lat * N_LON + my_lon, scale, small_out)
    stores.append(pltpu.make_async_copy(small_out, small_hbm, out_sem.at[9]))
    stores[-1].start()
    for copy in first + second + third:
        copy.wait_send()
    for each in (down, up):
        each.settle()
    for store in stores:
        store.wait()


def level(x, c, cov, wd, wu, kern, scale):
    hbm = pl.BlockSpec(memory_space=pl.ANY)
    wide = lambda rows: pltpu.VMEM((rows, WIDE, 128), F32)
    mat = lambda rows, cols=128: pltpu.VMEM((rows, cols), BF)
    dma = lambda n: pltpu.SemaphoreType.DMA((n,))
    tall = (ROWS + 1) * COLS
    planes = jax.ShapeDtypeStruct((64, 2, 2, ROWS, COLS), BF)
    scratch = (
        [mat(128, CELLS), mat(128, tall)] * 2
        + [mat(CELLS), mat(tall)] * 2
        + [mat(384, 256)] * 2
        + [pltpu.VMEM((ROWS, WIDE, 256), F32)] * 2
        + [wide(ROWS + 4), wide(ROWS + 2), wide(ROWS + 4), wide(ROWS + 2), wide(ROWS)]
        + [mat(tall, 256)] * 2
        + [pltpu.VMEM((4, REACH, 128), F32)]
        + [pltpu.VMEM((384, 128), F32)] * 2
        + [pltpu.VMEM((576, 128), F32)] * 2
        + [pltpu.VMEM((2, 1, 9), F32)]
        + [pltpu.VMEM((3, 16), jnp.int32), pltpu.VMEM((9, 64, 128), BF), pltpu.VMEM((9, 64, 128), BF)]
        + [pltpu.VMEM((9, 2, 128), F32)]
        + [pltpu.VMEM((4, 64, ROWS, COLS), BF)] * 2
        + [pltpu.VMEM((4, 64 * ROWS, COLS), F32)] * 2
        + [mat(384)] * 4
        + [mat(16)] * 2
        + [mat(128)] * 2
        + [pltpu.VMEM((200, 128), F32)] * 2
        + [mat(576)] * 4
        + [pltpu.VMEM((384, 256), F32), pltpu.VMEM((584, 128), F32), pltpu.VMEM((24, 128), F32)]
        + [dma(12), dma(11), dma(6), dma(6), dma(2), dma(2), dma(2), dma(2)]
        + sum_scratch()
        + sum_scratch()
    )
    return pl.pallas_call(
        functools.partial(kernel, scale),
        out_shape=(
            planes,
            planes,
            jax.ShapeDtypeStruct((576, 128), F32),
            jax.ShapeDtypeStruct((576, 128), F32),
            jax.ShapeDtypeStruct((2, 1, 9), F32),
        ),
        in_specs=[pl.BlockSpec(memory_space=pltpu.HBM)] * 6,
        out_specs=(hbm,) * 5,
        scratch_shapes=scratch,
        compiler_params=pltpu.CompilerParams(
            collective_id=0, has_side_effects=True, vmem_limit_bytes=46 * 1024 * 1024
        ),
        cost_estimate=pl.CostEstimate(flops=3_600_000_000, bytes_accessed=7_000_000, transcendentals=500_000),
    )(*(pltpu.with_memory_space_constraint(v, pltpu.HBM) for v in (x, c, cov, wd, wu, kern)))


def hand_on(*refs):
    count = len(refs) // 2
    sems = refs[-1]
    copies = [
        pltpu.make_async_copy(source, target, sems.at[n])
        for n, (source, target) in enumerate(zip(refs[:count], refs[count : 2 * count]))
    ]
    for copy in copies:
        copy.start()
    for copy in copies:
        copy.wait()


def handed_on(*arrays):
    vmem = pl.BlockSpec(memory_space=pltpu.VMEM)
    hbm = pl.BlockSpec(memory_space=pltpu.HBM)
    return pl.pallas_call(
        hand_on,
        out_shape=tuple(jax.ShapeDtypeStruct(a.shape, a.dtype) for a in arrays),
        in_specs=[vmem] * len(arrays),
        out_specs=(hbm,) * len(arrays),
        scratch_shapes=[pltpu.SemaphoreType.DMA((len(arrays),))],
        compiler_params=pltpu.CompilerParams(vmem_limit_bytes=16 * 1024 * 1024),
    )(*arrays)


def shards(inputs, kernels, w_down, w_up, cotangent, coverage):
    total = inputs.shape[3] * inputs.shape[4] * N_LAT * N_LON
    scale = 1.0 / math.sqrt(total)
    found = level(
        inputs,
        cotangent,
        coverage,
        jnp.transpose(w_down, (0, 2, 1)),
        w_up,
        jnp.transpose(kernels, (1, 0, 2)),
        scale,
    )
    decoded, grad_input, down, up, small = handed_on(*found)
    return (
        decoded,
        grad_input,
        jnp.transpose(down.reshape(9, 64, 128), (0, 2, 1)),
        up.reshape(9, 64, 128),
        jnp.transpose(small, (0, 2, 1)),
    )


def solution(mesh):
    placed = (
        P(None, None, None, "lat", "lon"),
        P(),
        P(),
        P(),
        P(None, None, None, "lat", "lon"),
        P("lat", "lon"),
    )
    return jax.shard_map(
        shards,
        mesh=mesh,
        in_specs=placed,
        out_specs=(
            P(None, None, None, "lat", "lon"),
            P(None, None, None, "lat", "lon"),
            P(),
            P(),
            P(None, None, ("lat", "lon")),
        ),
        check_vma=False,
    )
```

```python
import functools
import math

import jax
import jax.numpy as jnp
from jax import lax
from jax.experimental import pallas as pl
from jax.experimental.pallas import tpu as pltpu
from jax.sharding import PartitionSpec as P

BF = jnp.bfloat16
F32 = jnp.float32
ROWS = 24
COLS = 128
CELLS = ROWS * COLS
OFF = 16
WIDE = 160
LO = 8
SPAN = 144
REACH = 136
MESH = pl.DeviceIdType.MESH
N_LAT = 8
N_LON = 16
NEAR = 8
FAR = 16
PIECE = 72
PADDED = 80


def send(src, dst, send_sem, recv_sem, target):
    return pltpu.make_async_remote_copy(
        src_ref=src,
        dst_ref=dst,
        send_sem=send_sem,
        recv_sem=recv_sem,
        device_id=target,
        device_id_type=MESH,
    )


def greet(my_lat, my_lon):
    barrier = pltpu.get_barrier_semaphore()
    run, place, rank = my_lon // NEAR, lax.rem(my_lon, NEAR), my_lat * 2 + my_lon // NEAR
    peers = [(my_lat, run * NEAR + lax.rem(place + d, NEAR)) for d in range(1, NEAR)]
    for d in range(1, FAR):
        other = lax.rem(rank + d, FAR)
        peers.append((other // 2, lax.rem(other, 2) * NEAR + place))
    for side in (1, N_LON - 1):
        beside = lax.rem(my_lon + side, N_LON)
        peers += [(my_lat, beside), (lax.rem(my_lat + N_LAT - 1, N_LAT), beside)]
    for peer in peers:
        pl.semaphore_signal(barrier, inc=1, device_id=peer, device_id_type=MESH)
    return barrier, len(peers)


class Sum:
    def __init__(self, my_lat, my_lon, pieces, got, part, parts, whole, *sems):
        self.my_lat, self.run, self.place = my_lat, my_lon // NEAR, lax.rem(my_lon, NEAR)
        self.rank = my_lat * 2 + self.run
        self.pieces, self.got, self.part, self.parts, self.whole = pieces, got, part, parts, whole
        self.s1, self.r1, self.s2, self.r2, self.s3, self.r3 = sems

    def near(self, d):
        return (self.my_lat, self.run * NEAR + lax.rem(self.place + d, NEAR))

    def far(self, d):
        rank = lax.rem(self.rank + d, FAR)
        return (rank // 2, lax.rem(rank, 2) * NEAR + self.place)

    def first(self, d):
        peer = lax.rem(self.place + d, NEAR)
        return send(self.pieces.at[peer], self.got.at[d], self.s1, self.r1, self.near(d))

    def second(self, d):
        return send(self.part, self.parts.at[d], self.s2, self.r2, self.far(d))

    def third(self, d):
        return send(self.part, self.whole.at[d], self.s3, self.r3, self.near(d))

    def all_of(self, buffer, sent, received):
        arrived = buffer.at[pl.ds(1, buffer.shape[0] - 1)]
        return send(arrived, arrived, sent, received, self.near(1))

    def start_first(self):
        for d in range(1, NEAR):
            self.first(d).start()

    def start_second(self):
        self.all_of(self.got, self.s1, self.r1).wait_recv()
        total = self.pieces[self.place].astype(F32)
        for d in range(1, NEAR):
            total = total + self.got[d].astype(F32)
        rounded = total.astype(BF)
        self.part[...] = rounded
        self.parts[0] = rounded
        for d in range(1, FAR):
            self.second(d).start()

    def start_third(self):
        self.all_of(self.parts, self.s2, self.r2).wait()
        total = jnp.zeros((PADDED, 128), F32)
        for rank in range(FAR):
            total = total + self.parts[lax.rem(self.rank - rank + FAR, FAR)].astype(F32)
        rounded = total.astype(BF)
        self.part[...] = rounded
        self.whole[0] = rounded
        for d in range(1, NEAR):
            self.third(d).start()

    def extra(self, q):
        return self.whole[lax.rem(self.place - q + NEAR, NEAR)].astype(F32)[PIECE:]

    def finish(self, scale, out):
        self.all_of(self.whole, self.s3, self.r3).wait_recv()
        for d in range(NEAR):
            k = lax.rem(self.place - d + NEAR, NEAR)
            at = pl.ds(pl.multiple_of(k * PIECE, 8), PIECE)
            out[at, :] = self.whole[d].astype(F32)[:PIECE] * scale

    def settle(self):
        self.all_of(self.got, self.s1, self.r1).wait_send()
        self.all_of(self.whole, self.s3, self.r3).wait_send()


def sum_scratch():
    piece = lambda *lead: pltpu.VMEM(lead + (PADDED, 128), BF)
    buffers = [piece(NEAR), piece(NEAR), piece(), piece(FAR), piece(NEAR)]
    return buffers + [pltpu.SemaphoreType.DMA] * 6


def row_at(i):
    return pl.ds(pl.multiple_of(i * COLS, COLS), COLS)


def lay_weights(source, target):
    for a in range(3):
        top, mid, end = a * 128, a * 128 + 64, a * 128 + 128
        target[top:mid, 0:128] = source[3 * a + 1]
        target[mid:end, 0:128] = source[3 * a + 2]
        target[top:mid, 128:256] = jnp.zeros((64, 128), BF)
        target[mid:end, 128:256] = source[3 * a]


def own_channel(total, channel, scale, out):
    row = lax.broadcasted_iota(jnp.int32, total.shape, 0)
    lane = lax.broadcasted_iota(jnp.int32, total.shape, 1)
    column = jnp.sum(jnp.where(lane == channel, total, 0.0), axis=1, keepdims=True) * scale
    for t in range(2):
        line = jnp.sum(jnp.where(row == lane + 9 * t, column, 0.0), axis=0, keepdims=True)
        out[t] = line[:, 0:9]


def loop(low, high, body, wide=1):
    def step(n, carry):
        for k in range(wide):
            body(low + n * wide + k)
        return carry

    lax.fori_loop(0, (high - low) // wide, step, 0)


def plane_rows(i):
    return pl.ds(i, 64, stride=ROWS)


def taps_sum(field, coefs, first, rows_of, cols_of, span):
    total = None
    for a in range(3):
        for b in range(3):
            coef = coefs[3 * a + b, first : first + 1, :]
            term = coef * field[rows_of(a), pl.ds(cols_of(b), span), :]
            total = term if total is None else total + term
    return total


def kernel(
    scale, x_hbm, c_hbm, cov_hbm, wd_hbm, wu_hbm, kern_hbm,
    dec_hbm, gi_hbm, down_hbm, up_hbm, small_hbm,
    xa0, xa1, ma0, ma1, xb0, xb1, mb0, mb1, wdm, wum, yx, ym,
    s0, s1, r2, r1, ds_, d2, pg2, tmp, pack_l, pack_r,
    down_out, up_out, small_out, cov, wd, wu, kern, raw_x, raw_c, planes_x, planes_c, send_l, send_r, got_l, got_r, got_lc, got_rc, row_x, row_m,
    tile_l, tile_r, e2_up, e2_dn, got_up, got_dn, grad, flat, small_mine,
    in_sem, out_sem, e1_s, e1_r, e2_s, e2_r, e3_s, e3_r, *sums
):
    my_lat, my_lon = lax.axis_index("lat"), lax.axis_index("lon")
    up_lat, dn_lat = lax.rem(my_lat + N_LAT - 1, N_LAT), lax.rem(my_lat + 1, N_LAT)
    lt_lon, rt_lon = lax.rem(my_lon + N_LON - 1, N_LON), lax.rem(my_lon + 1, N_LON)
    has_up = (my_lat > 0).astype(F32)
    has_dn = (my_lat < N_LAT - 1).astype(F32)
    down = Sum(my_lat, my_lon, *sums[:11])
    up = Sum(my_lat, my_lon, *sums[11:22])

    loads = []
    for n, (source, raw) in enumerate(((x_hbm, raw_x), (c_hbm, raw_c))):
        for u in range(2):
            for v in range(2):
                p = 2 * u + v
                loads.append(
                    pltpu.make_async_copy(source.at[:, u, v], raw.at[p], in_sem.at[4 * n + p])
                )
    params = [
        pltpu.make_async_copy(source, target, in_sem.at[8 + n])
        for n, (source, target) in enumerate(
            ((cov_hbm, cov), (wd_hbm, wd), (wu_hbm, wu), (kern_hbm, kern))
        )
    ]
    for load in params + loads:
        load.start()
    barrier, met = greet(my_lat, my_lon)
    for load in params:
        load.wait()
    kern[4] = kern[4] + 1.0
    lay_weights(wd, wdm)
    lay_weights(wu, wum)
    spread = (
        lax.broadcasted_iota(jnp.int32, (16, COLS), 0)
        == lax.broadcasted_iota(jnp.int32, (16, COLS), 1) // 8
    ).astype(BF)
    flags = jnp.dot(cov[...].astype(F32).astype(BF), spread, preferred_element_type=F32).astype(BF)

    def unfold(raw, planes, p):
        def step(g):
            block = raw[p, pl.ds(g * 16, 16)].astype(F32)
            planes[p, pl.ds(pl.multiple_of(g * 384, 384), 384), :] = block.reshape(384, COLS)

        loop(0, 4, step)

    def turn(u, flag, planes, field, into, part, i):
        at = row_at(i + u)
        block = jnp.concatenate(
            [planes[2 * u, plane_rows(i), :], planes[2 * u + 1, plane_rows(i), :]], axis=0
        ).astype(BF)
        if flag is not None:
            block = block * flag
        field[:, at] = block
        block = block.T
        into[at, :] = block
        block = block.astype(F32)
        spot = u * 192 + i * 8 + part
        pack_l[pl.ds(spot, 4), :] = block[0:4]
        pack_r[pl.ds(spot, 4), :] = block[COLS - 4 : COLS]

    for u, field, into in ((0, xa0, xb0), (1, xa1, xb1)):
        for v in range(2):
            loads[2 * u + v].wait()
            unfold(raw_x, planes_x, 2 * u + v)
        loop(0, ROWS, functools.partial(turn, u, None, planes_x, field, into, 0), 12)
    for u, field, into in ((0, ma0, mb0), (1, ma1, mb1)):
        for v in range(2):
            loads[4 + 2 * u + v].wait()
            unfold(raw_c, planes_c, 2 * u + v)
        for q in range(3):
            body = functools.partial(turn, u, flags[q : q + 1, :], planes_c, field, into, 4)
            loop(8 * q, 8 * q + 8, body, 8)
    send_l[...] = pack_l[...].astype(BF)
    send_r[...] = pack_r[...].astype(BF)

    pl.semaphore_wait(barrier, met)
    last = pl.ds(ROWS * COLS, COLS)
    corner = pl.ds(368, 16)
    first = [
        send(send_l, got_r, e1_s.at[0], e1_r.at[0], (my_lat, lt_lon)),
        send(send_r, got_l, e1_s.at[1], e1_r.at[1], (my_lat, rt_lon)),
        send(send_l.at[corner], got_rc, e1_s.at[2], e1_r.at[2], (dn_lat, lt_lon)),
        send(send_r.at[corner], got_lc, e1_s.at[3], e1_r.at[3], (dn_lat, rt_lon)),
        send(xa1.at[:, last], row_x, e1_s.at[4], e1_r.at[4], (dn_lat, my_lon)),
        send(ma1.at[:, last], row_m, e1_s.at[5], e1_r.at[5], (dn_lat, my_lon)),
    ]
    for copy in first:
        copy.start()

    def conv_rows(i, count):
        here = pl.ds(pl.multiple_of(i * COLS, COLS), count * COLS)
        after = pl.ds(pl.multiple_of((i + 1) * COLS, COLS), count * COLS)
        for b0, b1, weight, y in ((xb0, xb1, wdm, yx), (mb0, mb1, wum, ym)):
            taps = jnp.concatenate([b1[here, :], b0[here, :], b1[after, :]], axis=1)
            found = jnp.dot(taps, weight[...], preferred_element_type=F32)
            for k in range(count):
                y[i + k, OFF : OFF + COLS, :] = found[k * COLS : (k + 1) * COLS]


    def activate(i, low=LO, count=SPAN):
        span, before = pl.ds(low, count), pl.ds(low - 1, count)
        pre = yx[i, span, 0:128] + yx[i, before, 128:256]
        sig = 0.5 * jnp.tanh(0.5 * pre) + 0.5
        s0[i + 2, span, :] = (pre * sig).astype(BF).astype(F32)
        ds_[i, span, :] = sig * (1.0 + pre * (1.0 - sig))
        grad_row = ym[i, span, 0:128] + ym[i, before, 128:256]
        r2[i + 2, span, :] = grad_row.astype(BF).astype(F32)

    def rims(i):
        activate(i, LO, 16)
        activate(i, OFF + COLS, 8)

    def activate_and_conv(n):
        for k in range(4):
            activate(4 * n - 4 + k)
        conv_rows(4 * n, 4)

    conv_rows(1, 3)
    loop(1, ROWS // 4, activate_and_conv)
    loop(ROWS - 4, ROWS, activate, 4)

    def forward_1(r, low=LO, count=SPAN):
        acc = taps_sum(s0, kern, 0, lambda a: r + a, lambda b: low - 1 + b, count)
        s1[r, pl.ds(low, count), :] = acc

    def backward_1(r, low=LO, count=SPAN):
        acc = taps_sum(r2, kern, 1, lambda a: r - a + 2, lambda b: low + 1 - b, count)
        r1[r, pl.ds(low, count), :] = acc

    def mend(r):
        for step in (forward_1, backward_1):
            step(r, LO, 16)
            step(r, LO + SPAN - 16, 16)

    loop(3, ROWS - 1, forward_1, 2)
    loop(3, ROWS - 1, backward_1, 2)


    for copy in first:
        copy.wait_recv()
    for got, field, into in ((row_x, xa1, xb1), (row_m, ma1, mb1)):
        row = got[...] * has_up.astype(BF)
        field[:, 0:COLS] = row
        into[0:COLS, :] = row.T
    conv_rows(0, 1)
    for got, edge, tile, at in ((got_l, got_lc, tile_l, 12), (got_r, got_rc, tile_r, 144)):
        tile[0:8, :] = edge[...].astype(F32)[8:16] * has_up
        tile[8:200, :] = got[192:384, :].astype(F32)
        taps = jnp.concatenate(
            [tile[0:192, :].astype(BF), got[0:192, :], tile[8:200, :].astype(BF)], axis=1
        )
        for weight, y, part in ((wdm, yx, 0), (wum, ym, 4)):
            rim = jnp.dot(taps, weight[...], preferred_element_type=F32)
            for i in range(ROWS):
                y[i, at : at + 4, :] = rim[i * 8 + part : i * 8 + part + 4]

    for i in (0, 1, ROWS - 2, ROWS - 1):
        rims(i) if i else activate(i)
    for n, field in enumerate((s0, r2)):
        for k in range(2):
            at = pl.ds(n * 288 + k * SPAN, SPAN)
            e2_up[at, :] = field[2 + k, LO : LO + SPAN, :].astype(BF)
            e2_dn[at, :] = field[ROWS + k, LO : LO + SPAN, :].astype(BF)
    second = [
        send(e2_up, got_up, e2_s.at[0], e2_r.at[0], (up_lat, my_lon)),
        send(e2_dn, got_dn, e2_s.at[1], e2_r.at[1], (dn_lat, my_lon)),
    ]
    for copy in second:
        copy.start()
    loop(2, ROWS - 2, rims, 4)

    loop(3, ROWS - 1, mend, 2)
    for r in (2, ROWS - 1):
        forward_1(r)
        backward_1(r)

    def pair(value, slot, into, i):
        slot = slot + lax.rem(i, 2)
        tmp[slot, 0:REACH, :] = value
        here = row_at(i)
        into[here, 0:128] = tmp[slot, 0:COLS, :].astype(BF)
        into[here, 128:256] = tmp[slot, 1 : COLS + 1, :].astype(BF)

    def backward_0(i):
        acc = taps_sum(r1, kern, 0, lambda a: i - a + 2, lambda b: OFF + 1 - b, REACH)
        value = acc.astype(BF).astype(F32) * ds_[i, pl.ds(OFF, REACH), :]
        pair(value, 0, pg2, i)

    def forward_0(i):
        acc = taps_sum(s1, kern, 1, lambda a: i + a, lambda b: OFF - 1 + b, REACH)
        pair(acc, 2, d2, i)

    loop(2, ROWS - 2, backward_0, 2)
    grad[...] = jnp.zeros_like(grad)

    def add_grad(a0, a1, pairs, row, count):
        at = pl.ds(pl.multiple_of(row * COLS, COLS), count * COLS)
        after = pl.ds(pl.multiple_of((row + 1) * COLS, COLS), count * COLS)
        taps = jnp.concatenate([a1[:, at], a0[:, at], a1[:, after]], axis=0)
        grad[...] += jnp.dot(taps, pairs[at, :], preferred_element_type=F32)

    def forward_and_grad(n):
        add_grad(xa0, xa1, pg2, 4 + 4 * n, 4)
        for k in range(5):
            forward_0(2 + 5 * n + k)

    loop(0, 4, forward_and_grad)
    for copy in second:
        copy.wait_recv()
    for n, field in enumerate((s0, r2)):
        for k in range(2):
            at = pl.ds(n * 288 + k * SPAN, SPAN)
            field[k, LO : LO + SPAN, :] = got_dn[at, :].astype(F32) * has_up
            field[ROWS + 2 + k, LO : LO + SPAN, :] = got_up[at, :].astype(F32) * has_dn
    def bound(field):
        field[0, LO : LO + SPAN, :] = field[0, LO : LO + SPAN, :] * has_up
        field[ROWS + 1, LO : LO + SPAN, :] = field[ROWS + 1, LO : LO + SPAN, :] * has_dn

    for r in (0, 1, ROWS, ROWS + 1):
        backward_1(r)
    bound(r1)

    for i in (0, 1, ROWS - 2, ROWS - 1):
        backward_0(i)
    third = [
        send(pg2.at[pl.ds(0, COLS)], pg2.at[pl.ds(CELLS, COLS)], e3_s.at[0], e3_r.at[0], (up_lat, my_lon)),
        send(d2.at[pl.ds(0, COLS)], d2.at[pl.ds(CELLS, COLS)], e3_s.at[1], e3_r.at[1], (up_lat, my_lon)),
    ]

    def lay_pieces(total):
        for a in range(3):
            top, mid, end = a * 128, a * 128 + 64, a * 128 + 128
            flat[(3 * a + 1) * 64 : (3 * a + 2) * 64, :] = grad[top:mid, 0:128]
            flat[(3 * a + 2) * 64 : (3 * a + 3) * 64, :] = grad[mid:end, 0:128]
            flat[3 * a * 64 : (3 * a + 1) * 64, :] = grad[mid:end, 128:256]
        for k in range(NEAR):
            total.pieces[k] = flat[pl.ds(k * PIECE, PADDED), :].astype(BF)

    flat[576:584, :] = jnp.zeros((8, 128), F32)
    small_mine[16:24, :] = jnp.zeros((8, 128), F32)
    add_grad(xa0, xa1, pg2, 0, 4)
    add_grad(xa0, xa1, pg2, ROWS - 4, 4)
    lay_pieces(down)
    down.start_first()
    for r in (0, 1, ROWS, ROWS + 1):
        forward_1(r)
    bound(s1)
    for i in (0, 1, ROWS - 2, ROWS - 1):
        forward_0(i)
    for copy in third:
        copy.start()

    def kernel_terms(own, other, accs):
        found = []
        for a in range(3):
            for b in range(3):
                near_by = other(a)[pl.ds(OFF - 1 + b, COLS), :]
                found.append(accs[3 * a + b] + jnp.sum((own * near_by).reshape(16, 8, 128), axis=0))
        return found

    def up_step(n, accs):
        add_grad(ma0, ma1, d2, 8 * n, 8)
        accs = list(accs)
        for k in range(8):
            i = 8 * n + k
            own = r1[i + 1, OFF : OFF + COLS, :]
            accs[:9] = kernel_terms(own, lambda a: s0.at[i + a + 1], accs[:9])
            own = r2[i + 2, OFF : OFF + COLS, :]
            accs[9:] = kernel_terms(own, lambda a: s1.at[i + a], accs[9:])
        return tuple(accs)

    grad[...] = jnp.zeros_like(grad)
    accs = lax.fori_loop(0, 3, up_step, tuple(jnp.zeros((8, 128), F32) for _ in range(18)))
    for t in range(18):
        small_mine[t : t + 1, :] = jnp.sum(accs[t], axis=0, keepdims=True)
    lay_pieces(up)
    for q in range(3):
        rows = flat[q * PIECE : (q + 1) * PIECE, :], small_mine[q * 8 : (q + 1) * 8, :]
        up.pieces[q] = jnp.concatenate(rows, axis=0).astype(BF)
    up.start_first()

    def add_piece(weight, pairs, f0, f1, planes, n):
        at = pl.ds(pl.multiple_of(n * 512, 512), 512)
        after = pl.ds(pl.multiple_of(n * 512 + COLS, COLS), 512)
        lines = jnp.concatenate([pairs[row_at(4 * n + k), :].T for k in range(5)], axis=1)
        found = jnp.dot(weight[128:384, :], lines[:, 0:512], preferred_element_type=F32)
        under = jnp.dot(weight[0:128, :], lines[:, COLS:640], preferred_element_type=F32)
        even = f0[:, at].astype(F32) + found[0:128]
        odd = f1[:, after].astype(F32) + found[128:256] + under
        for u, value in ((0, even), (1, odd)):
            for k in range(4):
                for v in range(2):
                    planes[2 * u + v, plane_rows(4 * n + k), :] = value[
                        v * 64 : (v + 1) * 64, k * COLS : (k + 1) * COLS
                    ]

    def put_out(planes, raw, out, sem):
        stores = []
        for u in range(2):
            for v in range(2):
                p = 2 * u + v

                def fold(g, p=p):
                    block = planes[p, pl.ds(pl.multiple_of(g * 384, 384), 384), :]
                    raw[p, pl.ds(g * 16, 16)] = block.astype(BF).reshape(16, ROWS, COLS)

                loop(0, 4, fold)
                stores.append(pltpu.make_async_copy(raw.at[p], out.at[:, u, v], sem.at[p]))
                stores[-1].start()
        return stores

    dec_piece = functools.partial(add_piece, wum, d2, xa0, xa1, planes_x)
    gi_piece = functools.partial(add_piece, wdm, pg2, ma0, ma1, planes_c)
    below = pl.ds(CELLS, COLS)

    loop(0, 1, dec_piece)
    down.start_second()
    for copy, field in zip(third, (pg2, d2)):
        copy.wait_recv()
        field[below, :] = field[below, :] * has_dn.astype(BF)
    loop(1, 6, dec_piece)
    stores = put_out(planes_x, raw_x, dec_hbm, out_sem)
    up.start_second()
    loop(0, 6, gi_piece)
    stores += put_out(planes_c, raw_c, gi_hbm, out_sem.at[pl.ds(4, 4)])
    down.start_third()
    up.start_third()
    down.finish(scale, down_out)
    stores.append(pltpu.make_async_copy(down_out, down_hbm, out_sem.at[8]))
    stores[-1].start()
    up.finish(scale, up_out)
    stores.append(pltpu.make_async_copy(up_out, up_hbm, out_sem.at[10]))
    stores[-1].start()
    for q in range(3):
        small_mine[q * 8 : (q + 1) * 8, :] = up.extra(q)
    own_channel(small_mine[...], my_lat * N_LON + my_lon, scale, small_out)
    stores.append(pltpu.make_async_copy(small_out, small_hbm, out_sem.at[9]))
    stores[-1].start()
    for copy in first + second + third:
        copy.wait_send()
    for each in (down, up):
        each.settle()
    for store in stores:
        store.wait()


def level(x, c, cov, wd, wu, kern, scale):
    hbm = pl.BlockSpec(memory_space=pl.ANY)
    wide = lambda rows: pltpu.VMEM((rows, WIDE, 128), F32)
    mat = lambda rows, cols=128: pltpu.VMEM((rows, cols), BF)
    dma = lambda n: pltpu.SemaphoreType.DMA((n,))
    tall = (ROWS + 1) * COLS
    planes = jax.ShapeDtypeStruct((64, 2, 2, ROWS, COLS), BF)
    scratch = (
        [mat(128, CELLS), mat(128, tall)] * 2
        + [mat(CELLS), mat(tall)] * 2
        + [mat(384, 256)] * 2
        + [pltpu.VMEM((ROWS, WIDE, 256), F32)] * 2
        + [wide(ROWS + 4), wide(ROWS + 2), wide(ROWS + 4), wide(ROWS + 2), wide(ROWS)]
        + [mat(tall, 256)] * 2
        + [pltpu.VMEM((4, REACH, 128), F32)]
        + [pltpu.VMEM((384, 128), F32)] * 2
        + [pltpu.VMEM((576, 128), F32)] * 2
        + [pltpu.VMEM((2, 1, 9), F32)]
        + [pltpu.VMEM((3, 16), jnp.int32), pltpu.VMEM((9, 64, 128), BF), pltpu.VMEM((9, 64, 128), BF)]
        + [pltpu.VMEM((9, 2, 128), F32)]
        + [pltpu.VMEM((4, 64, ROWS, COLS), BF)] * 2
        + [pltpu.VMEM((4, 64 * ROWS, COLS), F32)] * 2
        + [mat(384)] * 4
        + [mat(16)] * 2
        + [mat(128)] * 2
        + [pltpu.VMEM((200, 128), F32)] * 2
        + [mat(576)] * 4
        + [pltpu.VMEM((384, 256), F32), pltpu.VMEM((584, 128), F32), pltpu.VMEM((24, 128), F32)]
        + [dma(12), dma(11), dma(6), dma(6), dma(2), dma(2), dma(2), dma(2)]
        + sum_scratch()
        + sum_scratch()
    )
    return pl.pallas_call(
        functools.partial(kernel, scale),
        out_shape=(
            planes,
            planes,
            jax.ShapeDtypeStruct((576, 128), F32),
            jax.ShapeDtypeStruct((576, 128), F32),
            jax.ShapeDtypeStruct((2, 1, 9), F32),
        ),
        in_specs=[pl.BlockSpec(memory_space=pltpu.HBM)] * 6,
        out_specs=(hbm,) * 5,
        scratch_shapes=scratch,
        compiler_params=pltpu.CompilerParams(
            collective_id=0, has_side_effects=True, vmem_limit_bytes=46 * 1024 * 1024
        ),
        cost_estimate=pl.CostEstimate(flops=3_600_000_000, bytes_accessed=7_000_000, transcendentals=500_000),
    )(*(pltpu.with_memory_space_constraint(v, pltpu.HBM) for v in (x, c, cov, wd, wu, kern)))


def hand_on(*refs):
    count = len(refs) // 2
    sems = refs[-1]
    copies = [
        pltpu.make_async_copy(source, target, sems.at[n])
        for n, (source, target) in enumerate(zip(refs[:count], refs[count : 2 * count]))
    ]
    for copy in copies:
        copy.start()
    for copy in copies:
        copy.wait()


def handed_on(*arrays):
    vmem = pl.BlockSpec(memory_space=pltpu.VMEM)
    hbm = pl.BlockSpec(memory_space=pltpu.HBM)
    return pl.pallas_call(
        hand_on,
        out_shape=tuple(jax.ShapeDtypeStruct(a.shape, a.dtype) for a in arrays),
        in_specs=[vmem] * len(arrays),
        out_specs=(hbm,) * len(arrays),
        scratch_shapes=[pltpu.SemaphoreType.DMA((len(arrays),))],
        compiler_params=pltpu.CompilerParams(vmem_limit_bytes=16 * 1024 * 1024),
    )(*arrays)


def shards(inputs, kernels, w_down, w_up, cotangent, coverage):
    total = inputs.shape[3] * inputs.shape[4] * N_LAT * N_LON
    scale = 1.0 / math.sqrt(total)
    found = level(
        inputs,
        cotangent,
        coverage,
        jnp.transpose(w_down, (0, 2, 1)),
        w_up,
        jnp.transpose(kernels, (1, 0, 2)),
        scale,
    )
    decoded, grad_input, down, up, small = handed_on(*found)
    return (
        decoded,
        grad_input,
        jnp.transpose(down.reshape(9, 64, 128), (0, 2, 1)),
        up.reshape(9, 64, 128),
        jnp.transpose(small, (0, 2, 1)),
    )


def solution(mesh):
    placed = (
        P(None, None, None, "lat", "lon"),
        P(),
        P(),
        P(),
        P(None, None, None, "lat", "lon"),
        P("lat", "lon"),
    )
    return jax.shard_map(
        shards,
        mesh=mesh,
        in_specs=placed,
        out_specs=(
            P(None, None, None, "lat", "lon"),
            P(None, None, None, "lat", "lon"),
            P(),
            P(),
            P(None, None, ("lat", "lon")),
        ),
        check_vma=False,
    )
```

```python
import functools
import math

import jax
import jax.numpy as jnp
from jax import lax
from jax.experimental import pallas as pl
from jax.experimental.pallas import tpu as pltpu
from jax.sharding import PartitionSpec as P

BF = jnp.bfloat16
F32 = jnp.float32
ROWS = 24
COLS = 128
CELLS = ROWS * COLS
OFF = 16
WIDE = 160
LO = 8
SPAN = 144
REACH = 136
MESH = pl.DeviceIdType.MESH
N_LAT = 8
N_LON = 16
NEAR = 8
FAR = 16
PIECE = 72
PADDED = 80


def send(src, dst, send_sem, recv_sem, target):
    return pltpu.make_async_remote_copy(
        src_ref=src,
        dst_ref=dst,
        send_sem=send_sem,
        recv_sem=recv_sem,
        device_id=target,
        device_id_type=MESH,
    )


def greet(my_lat, my_lon):
    barrier = pltpu.get_barrier_semaphore()
    run, place, rank = my_lon // NEAR, lax.rem(my_lon, NEAR), my_lat * 2 + my_lon // NEAR
    peers = [(my_lat, run * NEAR + lax.rem(place + d, NEAR)) for d in range(1, NEAR)]
    for d in range(1, FAR):
        other = lax.rem(rank + d, FAR)
        peers.append((other // 2, lax.rem(other, 2) * NEAR + place))
    for side in (1, N_LON - 1):
        beside = lax.rem(my_lon + side, N_LON)
        peers += [(my_lat, beside), (lax.rem(my_lat + N_LAT - 1, N_LAT), beside)]
    for peer in peers:
        pl.semaphore_signal(barrier, inc=1, device_id=peer, device_id_type=MESH)
    return barrier, len(peers)


class Sum:
    def __init__(self, my_lat, my_lon, pieces, got, part, parts, whole, *sems):
        self.my_lat, self.run, self.place = my_lat, my_lon // NEAR, lax.rem(my_lon, NEAR)
        self.rank = my_lat * 2 + self.run
        self.pieces, self.got, self.part, self.parts, self.whole = pieces, got, part, parts, whole
        self.s1, self.r1, self.s2, self.r2, self.s3, self.r3 = sems

    def near(self, d):
        return (self.my_lat, self.run * NEAR + lax.rem(self.place + d, NEAR))

    def far(self, d):
        rank = lax.rem(self.rank + d, FAR)
        return (rank // 2, lax.rem(rank, 2) * NEAR + self.place)

    def first(self, d):
        peer = lax.rem(self.place + d, NEAR)
        return send(self.pieces.at[peer], self.got.at[d], self.s1, self.r1, self.near(d))

    def second(self, d):
        return send(self.part, self.parts.at[d], self.s2, self.r2, self.far(d))

    def third(self, d):
        return send(self.part, self.whole.at[d], self.s3, self.r3, self.near(d))

    def all_of(self, buffer, sent, received):
        arrived = buffer.at[pl.ds(1, buffer.shape[0] - 1)]
        return send(arrived, arrived, sent, received, self.near(1))

    def start_first(self):
        for d in range(1, NEAR):
            self.first(d).start()

    def start_second(self):
        self.all_of(self.got, self.s1, self.r1).wait_recv()
        total = self.pieces[self.place].astype(F32)
        for d in range(1, NEAR):
            total = total + self.got[d].astype(F32)
        rounded = total.astype(BF)
        self.part[...] = rounded
        self.parts[0] = rounded
        for d in range(1, FAR):
            self.second(d).start()

    def start_third(self):
        self.all_of(self.parts, self.s2, self.r2).wait()
        total = jnp.zeros((PADDED, 128), F32)
        for rank in range(FAR):
            total = total + self.parts[lax.rem(self.rank - rank + FAR, FAR)].astype(F32)
        rounded = total.astype(BF)
        self.part[...] = rounded
        self.whole[0] = rounded
        for d in range(1, NEAR):
            self.third(d).start()

    def extra(self, q):
        return self.whole[lax.rem(self.place - q + NEAR, NEAR)].astype(F32)[PIECE:]

    def finish(self, scale, out):
        self.all_of(self.whole, self.s3, self.r3).wait_recv()
        for d in range(NEAR):
            k = lax.rem(self.place - d + NEAR, NEAR)
            at = pl.ds(pl.multiple_of(k * PIECE, 8), PIECE)
            out[at, :] = self.whole[d].astype(F32)[:PIECE] * scale

    def settle(self):
        self.all_of(self.got, self.s1, self.r1).wait_send()
        self.all_of(self.whole, self.s3, self.r3).wait_send()


def sum_scratch():
    piece = lambda *lead: pltpu.VMEM(lead + (PADDED, 128), BF)
    buffers = [piece(NEAR), piece(NEAR), piece(), piece(FAR), piece(NEAR)]
    return buffers + [pltpu.SemaphoreType.DMA] * 6


def row_at(i):
    return pl.ds(pl.multiple_of(i * COLS, COLS), COLS)


def lay_weights(source, target):
    for a in range(3):
        top, mid, end = a * 128, a * 128 + 64, a * 128 + 128
        target[top:mid, 0:128] = source[3 * a + 1]
        target[mid:end, 0:128] = source[3 * a + 2]
        target[top:mid, 128:256] = jnp.zeros((64, 128), BF)
        target[mid:end, 128:256] = source[3 * a]


def own_channel(total, channel, scale, out):
    row = lax.broadcasted_iota(jnp.int32, total.shape, 0)
    lane = lax.broadcasted_iota(jnp.int32, total.shape, 1)
    column = jnp.sum(jnp.where(lane == channel, total, 0.0), axis=1, keepdims=True) * scale
    for t in range(2):
        line = jnp.sum(jnp.where(row == lane + 9 * t, column, 0.0), axis=0, keepdims=True)
        out[t] = line[:, 0:9]


def loop(low, high, body, wide=1):
    def step(n, carry):
        for k in range(wide):
            body(low + n * wide + k)
        return carry

    lax.fori_loop(0, (high - low) // wide, step, 0)


def plane_rows(i):
    return pl.ds(i, 64, stride=ROWS)


def taps_sum(field, coefs, first, rows_of, cols_of, span):
    total = None
    for a in range(3):
        for b in range(3):
            coef = coefs[3 * a + b, first : first + 1, :]
            term = coef * field[rows_of(a), pl.ds(cols_of(b), span), :]
            total = term if total is None else total + term
    return total


def kernel(
    scale, x_hbm, c_hbm, cov_hbm, wd_hbm, wu_hbm, kern_hbm,
    dec_hbm, gi_hbm, down_hbm, up_hbm, small_hbm,
    xa0, xa1, ma0, ma1, xb0, xb1, mb0, mb1, wdm, wum, yx, ym,
    s0, s1, r2, r1, ds_, d2, pg2, tmp, pack_l, pack_r,
    down_out, up_out, small_out, cov, wd, wu, kern, raw_x, raw_c, planes_x, planes_c, send_l, send_r, got_l, got_r, got_lc, got_rc, row_x, row_m,
    tile_l, tile_r, e2_up, e2_dn, got_up, got_dn, grad, flat, small_mine,
    in_sem, out_sem, e1_s, e1_r, e2_s, e2_r, e3_s, e3_r, *sums
):
    my_lat, my_lon = lax.axis_index("lat"), lax.axis_index("lon")
    up_lat, dn_lat = lax.rem(my_lat + N_LAT - 1, N_LAT), lax.rem(my_lat + 1, N_LAT)
    lt_lon, rt_lon = lax.rem(my_lon + N_LON - 1, N_LON), lax.rem(my_lon + 1, N_LON)
    has_up = (my_lat > 0).astype(F32)
    has_dn = (my_lat < N_LAT - 1).astype(F32)
    down = Sum(my_lat, my_lon, *sums[:11])
    up = Sum(my_lat, my_lon, *sums[11:22])

    loads = []
    for n, (source, raw) in enumerate(((x_hbm, raw_x), (c_hbm, raw_c))):
        for u in range(2):
            for v in range(2):
                p = 2 * u + v
                loads.append(
                    pltpu.make_async_copy(source.at[:, u, v], raw.at[p], in_sem.at[4 * n + p])
                )
    params = [
        pltpu.make_async_copy(source, target, in_sem.at[8 + n])
        for n, (source, target) in enumerate(
            ((cov_hbm, cov), (wd_hbm, wd), (wu_hbm, wu), (kern_hbm, kern))
        )
    ]
    for load in params + loads:
        load.start()
    barrier, met = greet(my_lat, my_lon)
    for load in params:
        load.wait()
    kern[4] = kern[4] + 1.0
    lay_weights(wd, wdm)
    lay_weights(wu, wum)
    spread = (
        lax.broadcasted_iota(jnp.int32, (16, COLS), 0)
        == lax.broadcasted_iota(jnp.int32, (16, COLS), 1) // 8
    ).astype(BF)
    flags = jnp.dot(cov[...].astype(F32).astype(BF), spread, preferred_element_type=F32).astype(BF)

    def unfold(raw, planes, p):
        def step(g):
            block = raw[p, pl.ds(g * 16, 16)].astype(F32)
            planes[p, pl.ds(pl.multiple_of(g * 384, 384), 384), :] = block.reshape(384, COLS)

        loop(0, 4, step)

    def turn(u, flag, planes, field, into, part, i):
        at = row_at(i + u)
        block = jnp.concatenate(
            [planes[2 * u, plane_rows(i), :], planes[2 * u + 1, plane_rows(i), :]], axis=0
        ).astype(BF)
        if flag is not None:
            block = block * flag
        field[:, at] = block
        block = block.T
        into[at, :] = block
        block = block.astype(F32)
        spot = u * 192 + i * 8 + part
        pack_l[pl.ds(spot, 4), :] = block[0:4]
        pack_r[pl.ds(spot, 4), :] = block[COLS - 4 : COLS]

    for u, field, into in ((0, xa0, xb0), (1, xa1, xb1)):
        for v in range(2):
            loads[2 * u + v].wait()
            unfold(raw_x, planes_x, 2 * u + v)
        loop(0, ROWS, functools.partial(turn, u, None, planes_x, field, into, 0), 12)
    for u, field, into in ((0, ma0, mb0), (1, ma1, mb1)):
        for v in range(2):
            loads[4 + 2 * u + v].wait()
            unfold(raw_c, planes_c, 2 * u + v)
        for q in range(3):
            body = functools.partial(turn, u, flags[q : q + 1, :], planes_c, field, into, 4)
            loop(8 * q, 8 * q + 8, body, 8)
    send_l[...] = pack_l[...].astype(BF)
    send_r[...] = pack_r[...].astype(BF)

    pl.semaphore_wait(barrier, met)
    last = pl.ds(ROWS * COLS, COLS)
    corner = pl.ds(368, 16)
    first = [
        send(send_l, got_r, e1_s.at[0], e1_r.at[0], (my_lat, lt_lon)),
        send(send_r, got_l, e1_s.at[1], e1_r.at[1], (my_lat, rt_lon)),
        send(send_l.at[corner], got_rc, e1_s.at[2], e1_r.at[2], (dn_lat, lt_lon)),
        send(send_r.at[corner], got_lc, e1_s.at[3], e1_r.at[3], (dn_lat, rt_lon)),
        send(xa1.at[:, last], row_x, e1_s.at[4], e1_r.at[4], (dn_lat, my_lon)),
        send(ma1.at[:, last], row_m, e1_s.at[5], e1_r.at[5], (dn_lat, my_lon)),
    ]
    for copy in first:
        copy.start()

    def conv_rows(i, count):
        here = pl.ds(pl.multiple_of(i * COLS, COLS), count * COLS)
        after = pl.ds(pl.multiple_of((i + 1) * COLS, COLS), count * COLS)
        for b0, b1, weight, y in ((xb0, xb1, wdm, yx), (mb0, mb1, wum, ym)):
            taps = jnp.concatenate([b1[here, :], b0[here, :], b1[after, :]], axis=1)
            found = jnp.dot(taps, weight[...], preferred_element_type=F32)
            for k in range(count):
                y[i + k, OFF : OFF + COLS, :] = found[k * COLS : (k + 1) * COLS]


    def activate(i, low=LO, count=SPAN):
        span, before = pl.ds(low, count), pl.ds(low - 1, count)
        pre = yx[i, span, 0:128] + yx[i, before, 128:256]
        sig = 0.5 * jnp.tanh(0.5 * pre) + 0.5
        s0[i + 2, span, :] = (pre * sig).astype(BF).astype(F32)
        ds_[i, span, :] = sig * (1.0 + pre * (1.0 - sig))
        grad_row = ym[i, span, 0:128] + ym[i, before, 128:256]
        r2[i + 2, span, :] = grad_row.astype(BF).astype(F32)

    def rims(i):
        activate(i, LO, 16)
        activate(i, OFF + COLS, 8)

    def activate_and_conv(n):
        for k in range(4):
            activate(4 * n - 4 + k)
        conv_rows(4 * n, 4)

    conv_rows(1, 3)
    loop(1, ROWS // 4, activate_and_conv)
    loop(ROWS - 4, ROWS, activate, 4)

    def forward_1(r, low=LO, count=SPAN):
        acc = taps_sum(s0, kern, 0, lambda a: r + a, lambda b: low - 1 + b, count)
        s1[r, pl.ds(low, count), :] = acc

    def backward_1(r, low=LO, count=SPAN):
        acc = taps_sum(r2, kern, 1, lambda a: r - a + 2, lambda b: low + 1 - b, count)
        r1[r, pl.ds(low, count), :] = acc

    def mend(r):
        for step in (forward_1, backward_1):
            step(r, LO, 16)
            step(r, LO + SPAN - 16, 16)

    loop(3, ROWS - 1, forward_1, 2)
    loop(3, ROWS - 1, backward_1, 2)


    for copy in first:
        copy.wait_recv()
    for got, field, into in ((row_x, xa1, xb1), (row_m, ma1, mb1)):
        row = got[...] * has_up.astype(BF)
        field[:, 0:COLS] = row
        into[0:COLS, :] = row.T
    conv_rows(0, 1)
    for got, edge, tile, at in ((got_l, got_lc, tile_l, 12), (got_r, got_rc, tile_r, 144)):
        tile[0:8, :] = edge[...].astype(F32)[8:16] * has_up
        tile[8:200, :] = got[192:384, :].astype(F32)
        taps = jnp.concatenate(
            [tile[0:192, :].astype(BF), got[0:192, :], tile[8:200, :].astype(BF)], axis=1
        )
        for weight, y, part in ((wdm, yx, 0), (wum, ym, 4)):
            rim = jnp.dot(taps, weight[...], preferred_element_type=F32)
            for i in range(ROWS):
                y[i, at : at + 4, :] = rim[i * 8 + part : i * 8 + part + 4]

    for i in (0, 1, ROWS - 2, ROWS - 1):
        rims(i) if i else activate(i)
    for n, field in enumerate((s0, r2)):
        for k in range(2):
            at = pl.ds(n * 288 + k * SPAN, SPAN)
            e2_up[at, :] = field[2 + k, LO : LO + SPAN, :].astype(BF)
            e2_dn[at, :] = field[ROWS + k, LO : LO + SPAN, :].astype(BF)
    second = [
        send(e2_up, got_up, e2_s.at[0], e2_r.at[0], (up_lat, my_lon)),
        send(e2_dn, got_dn, e2_s.at[1], e2_r.at[1], (dn_lat, my_lon)),
    ]
    for copy in second:
        copy.start()
    loop(2, ROWS - 2, rims, 4)

    loop(3, ROWS - 1, mend, 2)
    for r in (2, ROWS - 1):
        forward_1(r)
        backward_1(r)

    def pair(value, slot, into, i):
        slot = slot + lax.rem(i, 2)
        tmp[slot, 0:REACH, :] = value
        here = row_at(i)
        into[here, 0:128] = tmp[slot, 0:COLS, :].astype(BF)
        into[here, 128:256] = tmp[slot, 1 : COLS + 1, :].astype(BF)

    def backward_0(i):
        acc = taps_sum(r1, kern, 0, lambda a: i - a + 2, lambda b: OFF + 1 - b, REACH)
        value = acc.astype(BF).astype(F32) * ds_[i, pl.ds(OFF, REACH), :]
        pair(value, 0, pg2, i)

    def forward_0(i):
        acc = taps_sum(s1, kern, 1, lambda a: i + a, lambda b: OFF - 1 + b, REACH)
        pair(acc, 2, d2, i)

    loop(2, ROWS - 2, backward_0, 2)
    grad[...] = jnp.zeros_like(grad)

    def add_grad(a0, a1, pairs, row, count):
        at = pl.ds(pl.multiple_of(row * COLS, COLS), count * COLS)
        after = pl.ds(pl.multiple_of((row + 1) * COLS, COLS), count * COLS)
        taps = jnp.concatenate([a1[:, at], a0[:, at], a1[:, after]], axis=0)
        grad[...] += jnp.dot(taps, pairs[at, :], preferred_element_type=F32)

    def forward_and_grad(n):
        add_grad(xa0, xa1, pg2, 4 + 4 * n, 4)
        for k in range(5):
            forward_0(2 + 5 * n + k)

    loop(0, 4, forward_and_grad)
    for copy in second:
        copy.wait_recv()
    for n, field in enumerate((s0, r2)):
        for k in range(2):
            at = pl.ds(n * 288 + k * SPAN, SPAN)
            field[k, LO : LO + SPAN, :] = got_dn[at, :].astype(F32) * has_up
            field[ROWS + 2 + k, LO : LO + SPAN, :] = got_up[at, :].astype(F32) * has_dn
    def bound(field):
        field[0, LO : LO + SPAN, :] = field[0, LO : LO + SPAN, :] * has_up
        field[ROWS + 1, LO : LO + SPAN, :] = field[ROWS + 1, LO : LO + SPAN, :] * has_dn

    for r in (0, 1, ROWS, ROWS + 1):
        backward_1(r)
    bound(r1)

    for i in (0, 1, ROWS - 2, ROWS - 1):
        backward_0(i)
    third = [
        send(pg2.at[pl.ds(0, COLS)], pg2.at[pl.ds(CELLS, COLS)], e3_s.at[0], e3_r.at[0], (up_lat, my_lon)),
        send(d2.at[pl.ds(0, COLS)], d2.at[pl.ds(CELLS, COLS)], e3_s.at[1], e3_r.at[1], (up_lat, my_lon)),
    ]

    def lay_pieces(total):
        for a in range(3):
            top, mid, end = a * 128, a * 128 + 64, a * 128 + 128
            flat[(3 * a + 1) * 64 : (3 * a + 2) * 64, :] = grad[top:mid, 0:128]
            flat[(3 * a + 2) * 64 : (3 * a + 3) * 64, :] = grad[mid:end, 0:128]
            flat[3 * a * 64 : (3 * a + 1) * 64, :] = grad[mid:end, 128:256]
        for k in range(NEAR):
            total.pieces[k] = flat[pl.ds(k * PIECE, PADDED), :].astype(BF)

    flat[576:584, :] = jnp.zeros((8, 128), F32)
    small_mine[16:24, :] = jnp.zeros((8, 128), F32)
    add_grad(xa0, xa1, pg2, 0, 4)
    add_grad(xa0, xa1, pg2, ROWS - 4, 4)
    lay_pieces(down)
    down.start_first()
    for r in (0, 1, ROWS, ROWS + 1):
        forward_1(r)
    bound(s1)
    for i in (0, 1, ROWS - 2, ROWS - 1):
        forward_0(i)
    for copy in third:
        copy.start()

    def kernel_terms(own, other, accs):
        found = []
        for a in range(3):
            for b in range(3):
                near_by = other(a)[pl.ds(OFF - 1 + b, COLS), :]
                found.append(accs[3 * a + b] + jnp.sum((own * near_by).reshape(16, 8, 128), axis=0))
        return found

    def up_step(n, accs):
        add_grad(ma0, ma1, d2, 8 * n, 8)
        accs = list(accs)
        for k in range(8):
            i = 8 * n + k
            own = r1[i + 1, OFF : OFF + COLS, :]
            accs[:9] = kernel_terms(own, lambda a: s0.at[i + a + 1], accs[:9])
            own = r2[i + 2, OFF : OFF + COLS, :]
            accs[9:] = kernel_terms(own, lambda a: s1.at[i + a], accs[9:])
        return tuple(accs)

    grad[...] = jnp.zeros_like(grad)
    accs = lax.fori_loop(0, 3, up_step, tuple(jnp.zeros((8, 128), F32) for _ in range(18)))
    for t in range(18):
        small_mine[t : t + 1, :] = jnp.sum(accs[t], axis=0, keepdims=True)
    lay_pieces(up)
    for q in range(3):
        rows = flat[q * PIECE : (q + 1) * PIECE, :], small_mine[q * 8 : (q + 1) * 8, :]
        up.pieces[q] = jnp.concatenate(rows, axis=0).astype(BF)
    up.start_first()

    def add_piece(weight, pairs, f0, f1, planes, n):
        at = pl.ds(pl.multiple_of(n * 512, 512), 512)
        after = pl.ds(pl.multiple_of(n * 512 + COLS, COLS), 512)
        lines = jnp.concatenate([pairs[row_at(4 * n + k), :].T for k in range(5)], axis=1)
        found = jnp.dot(weight[128:384, :], lines[:, 0:512], preferred_element_type=F32)
        under = jnp.dot(weight[0:128, :], lines[:, COLS:640], preferred_element_type=F32)
        even = f0[:, at].astype(F32) + found[0:128]
        odd = f1[:, after].astype(F32) + found[128:256] + under
        for u, value in ((0, even), (1, odd)):
            for k in range(4):
                for v in range(2):
                    planes[2 * u + v, plane_rows(4 * n + k), :] = value[
                        v * 64 : (v + 1) * 64, k * COLS : (k + 1) * COLS
                    ]

    def put_out(planes, raw, out, sem):
        stores = []
        for u in range(2):
            for v in range(2):
                p = 2 * u + v

                def fold(g, p=p):
                    block = planes[p, pl.ds(pl.multiple_of(g * 384, 384), 384), :]
                    raw[p, pl.ds(g * 16, 16)] = block.astype(BF).reshape(16, ROWS, COLS)

                loop(0, 4, fold)
                stores.append(pltpu.make_async_copy(raw.at[p], out.at[:, u, v], sem.at[p]))
                stores[-1].start()
        return stores

    dec_piece = functools.partial(add_piece, wum, d2, xa0, xa1, planes_x)
    gi_piece = functools.partial(add_piece, wdm, pg2, ma0, ma1, planes_c)
    below = pl.ds(CELLS, COLS)

    loop(0, 2, dec_piece)
    down.start_second()
    loop(2, 5, dec_piece)
    up.start_second()
    for copy, field in zip(third, (pg2, d2)):
        copy.wait_recv()
        field[below, :] = field[below, :] * has_dn.astype(BF)
    loop(5, 6, dec_piece)
    stores = put_out(planes_x, raw_x, dec_hbm, out_sem)
    loop(0, 4, gi_piece)
    down.start_third()
    loop(4, 6, gi_piece)
    stores += put_out(planes_c, raw_c, gi_hbm, out_sem.at[pl.ds(4, 4)])
    up.start_third()
    down.finish(scale, down_out)
    stores.append(pltpu.make_async_copy(down_out, down_hbm, out_sem.at[8]))
    stores[-1].start()
    up.finish(scale, up_out)
    stores.append(pltpu.make_async_copy(up_out, up_hbm, out_sem.at[10]))
    stores[-1].start()
    for q in range(3):
        small_mine[q * 8 : (q + 1) * 8, :] = up.extra(q)
    own_channel(small_mine[...], my_lat * N_LON + my_lon, scale, small_out)
    stores.append(pltpu.make_async_copy(small_out, small_hbm, out_sem.at[9]))
    stores[-1].start()
    for copy in first + second + third:
        copy.wait_send()
    for each in (down, up):
        each.settle()
    for store in stores:
        store.wait()


def level(x, c, cov, wd, wu, kern, scale):
    hbm = pl.BlockSpec(memory_space=pl.ANY)
    wide = lambda rows: pltpu.VMEM((rows, WIDE, 128), F32)
    mat = lambda rows, cols=128: pltpu.VMEM((rows, cols), BF)
    dma = lambda n: pltpu.SemaphoreType.DMA((n,))
    tall = (ROWS + 1) * COLS
    planes = jax.ShapeDtypeStruct((64, 2, 2, ROWS, COLS), BF)
    scratch = (
        [mat(128, CELLS), mat(128, tall)] * 2
        + [mat(CELLS), mat(tall)] * 2
        + [mat(384, 256)] * 2
        + [pltpu.VMEM((ROWS, WIDE, 256), F32)] * 2
        + [wide(ROWS + 4), wide(ROWS + 2), wide(ROWS + 4), wide(ROWS + 2), wide(ROWS)]
        + [mat(tall, 256)] * 2
        + [pltpu.VMEM((4, REACH, 128), F32)]
        + [pltpu.VMEM((384, 128), F32)] * 2
        + [pltpu.VMEM((576, 128), F32)] * 2
        + [pltpu.VMEM((2, 1, 9), F32)]
        + [pltpu.VMEM((3, 16), jnp.int32), pltpu.VMEM((9, 64, 128), BF), pltpu.VMEM((9, 64, 128), BF)]
        + [pltpu.VMEM((9, 2, 128), F32)]
        + [pltpu.VMEM((4, 64, ROWS, COLS), BF)] * 2
        + [pltpu.VMEM((4, 64 * ROWS, COLS), F32)] * 2
        + [mat(384)] * 4
        + [mat(16)] * 2
        + [mat(128)] * 2
        + [pltpu.VMEM((200, 128), F32)] * 2
        + [mat(576)] * 4
        + [pltpu.VMEM((384, 256), F32), pltpu.VMEM((584, 128), F32), pltpu.VMEM((24, 128), F32)]
        + [dma(12), dma(11), dma(6), dma(6), dma(2), dma(2), dma(2), dma(2)]
        + sum_scratch()
        + sum_scratch()
    )
    return pl.pallas_call(
        functools.partial(kernel, scale),
        out_shape=(
            planes,
            planes,
            jax.ShapeDtypeStruct((576, 128), F32),
            jax.ShapeDtypeStruct((576, 128), F32),
            jax.ShapeDtypeStruct((2, 1, 9), F32),
        ),
        in_specs=[pl.BlockSpec(memory_space=pltpu.HBM)] * 6,
        out_specs=(hbm,) * 5,
        scratch_shapes=scratch,
        compiler_params=pltpu.CompilerParams(
            collective_id=0, has_side_effects=True, vmem_limit_bytes=46 * 1024 * 1024
        ),
        cost_estimate=pl.CostEstimate(flops=3_600_000_000, bytes_accessed=7_000_000, transcendentals=500_000),
    )(*(pltpu.with_memory_space_constraint(v, pltpu.HBM) for v in (x, c, cov, wd, wu, kern)))


def hand_on(*refs):
    count = len(refs) // 2
    sems = refs[-1]
    copies = []
    for n, (source, target) in enumerate(zip(refs[:count], refs[count : 2 * count])):
        parts = 4 if n < 2 else 1
        size = source.shape[0] // parts
        for k in range(parts):
            at = pl.ds(k * size, size)
            copies.append(pltpu.make_async_copy(source.at[at], target.at[at], sems.at[4 * n + k]))
    for copy in copies:
        copy.start()
    for copy in copies:
        copy.wait()


def handed_on(*arrays):
    vmem = pl.BlockSpec(memory_space=pltpu.VMEM)
    hbm = pl.BlockSpec(memory_space=pltpu.HBM)
    return pl.pallas_call(
        hand_on,
        out_shape=tuple(jax.ShapeDtypeStruct(a.shape, a.dtype) for a in arrays),
        in_specs=[vmem] * len(arrays),
        out_specs=(hbm,) * len(arrays),
        scratch_shapes=[pltpu.SemaphoreType.DMA((4 * len(arrays),))],
        compiler_params=pltpu.CompilerParams(vmem_limit_bytes=16 * 1024 * 1024),
    )(*arrays)


def shards(inputs, kernels, w_down, w_up, cotangent, coverage):
    total = inputs.shape[3] * inputs.shape[4] * N_LAT * N_LON
    scale = 1.0 / math.sqrt(total)
    found = level(
        inputs,
        cotangent,
        coverage,
        jnp.transpose(w_down, (0, 2, 1)),
        w_up,
        jnp.transpose(kernels, (1, 0, 2)),
        scale,
    )
    decoded, grad_input, down, up, small = handed_on(*found)
    return (
        decoded,
        grad_input,
        jnp.transpose(down.reshape(9, 64, 128), (0, 2, 1)),
        up.reshape(9, 64, 128),
        jnp.transpose(small, (0, 2, 1)),
    )


def solution(mesh):
    placed = (
        P(None, None, None, "lat", "lon"),
        P(),
        P(),
        P(),
        P(None, None, None, "lat", "lon"),
        P("lat", "lon"),
    )
    return jax.shard_map(
        shards,
        mesh=mesh,
        in_specs=placed,
        out_specs=(
            P(None, None, None, "lat", "lon"),
            P(None, None, None, "lat", "lon"),
            P(),
            P(),
            P(None, None, ("lat", "lon")),
        ),
        check_vma=False,
    )
```
